256 devices in a mesh: pole: 4 (over x), row: 16 (over z, core), col: 4 (over y).
Axes of the slice: x: 4, y: 4, z: 8, core: 2. Of those that a mesh axis runs over, the one named last changes fastest.
Arguments:
- lower_one: bfloat16 [4, 2, 1, 1024, 1024], P('pole', None, None, 'row', 'col'), may hold values from -0.125 to 0.125
- lower_two: bfloat16 [4, 4, 2, 1024, 1024], P('pole', None, None, 'row', 'col'), may hold values from -0.09375 to 0.09375
- lower_three: bfloat16 [4, 8, 3, 1024, 1024], P('pole', None, None, 'row', 'col'), may hold values from -0.078125 to 0.078125
- diag_inverse: bfloat16 [4, 15, 1024, 1024], P('pole', None, 'row', 'col'), as said below
- pole_weight: float32 [4], P('pole'), may hold values from 0.3 to 3
- super_sizes: int32 [15, 2], replicated, may hold values from 128 to 512, as said below
- parents: int32 [12], replicated, may hold values from 0 to 3, as said below
- keep_two: int32 [4], replicated, may hold values 0 or 1
- keep_three: int32 [8, 2], replicated, may hold values 0 or 1
Outputs:
- density_top: float32 [5, 1024, 1024], P(None, 'row', 'col')
- density_two: float32 [4, 3, 1024, 1024], P('pole', None, 'row', 'col')
- density_three: float32 [8, 4, 1024, 1024], P('pole', None, 'row', 'col')
The draws below stay inside these ranges and needn't reach their ends.
Inputs may be any that keep to these rules, and one draw needn't show every extreme that they name: `super_sizes`: each tree node's block of 1024 rows holds 2 supernodes of up to 512 rows each; the largest and the smallest size occur in every draw. `parents`: entries 0 to 3 each lie in 0 to 1, and each level-one node is named by exactly two of them; entries 4 to 11 each lie in 0 to 3, and each level-two node is named by exactly two of them. Each block diag_inverse[p, k] is symmetric.
All inputs are finite; a program needn't handle non-finite values.
Results may differ from the reference program's by a relative error of at most 0.0035.
Values may be sent and summed in bfloat16 or wider, within the bound.
A program may use at most 128 MiB of HBM per device.

```python
import math
import jax
import jax.numpy as jnp
from jax import lax

SUPB = 512
NSUP = 2
W = 1024
NODES = 15
POLES = 4


def draw_diag_inverse(key, part):
    key = jax.random.fold_in(key, 11)
    base = jax.random.normal(key, (POLES, NODES, W, W), jnp.float32)
    return ((base + jnp.swapaxes(base, 2, 3)) * 0.70710678).astype(jnp.bfloat16)


def draw_super_sizes(key, part):
    key = jax.random.fold_in(key, 23)
    first, second = jax.random.split(key, 2)
    values = jax.random.randint(first, (NODES * NSUP,), SUPB // 4, SUPB + 1)
    order = jax.random.permutation(second, NODES * NSUP)
    values = jnp.where(order == 0, SUPB, values)
    values = jnp.where(order == 1, SUPB // 4, values)
    return values.reshape(NODES, NSUP).astype(jnp.int32)


def draw_parents(key, part):
    key = jax.random.fold_in(key, 37)
    first, second = jax.random.split(key, 2)
    upper = jax.random.permutation(first, 4) // 2
    lower = jax.random.permutation(second, 8) // 2
    return jnp.concatenate([upper, lower], axis=0).astype(jnp.int32)


def plant(values, rng, smallest, high):
    shape = values.shape
    place = [jax.random.randint(jax.random.fold_in(rng, axis), (), 0, shape[axis]) for axis in range(len(shape))]
    values = values.at[tuple(place)].set(smallest)
    longest = shape.index(max(shape))
    place[longest] = (place[longest] + 1) % shape[longest]
    return values.at[tuple(place)].set(high)


def steps_of(stream_key, dims, cuts, low, high):
    gain = 1.0
    for dim, shards_of in cuts:
        draws = jax.random.uniform(jax.random.fold_in(jax.random.fold_in(stream_key, 6), dim), (shards_of,), jnp.float32, low / len(cuts), high / len(cuts))
        gain = gain * jnp.repeat(jnp.exp(draws), dims[dim] // shards_of).reshape((-1,) + (1,) * (len(dims) - 1 - dim))
    return gain


def bell_draw(own_key, extent, width, most, pieces=(), kind=jnp.bfloat16):
    array = width * jax.random.normal(own_key, extent, jnp.float32)
    if pieces:
        array = array * steps_of(own_key, extent, pieces, -0.22, 0.18)
    return jnp.clip(array, -most, most).astype(kind)


def setup_inputs(seed: int = 0) -> dict:
    key_list = jax.random.split(jax.random.key(seed), 10)
    lower_one = bell_draw(key_list[0], (POLES, 2, 1, W, W), (2 * W) ** -0.5, 0.125, ((0, 4), (3, 16), (4, 4)))
    lower_two = bell_draw(key_list[1], (POLES, 4, 2, W, W), (4 * W) ** -0.5, 0.09375, ((0, 4), (3, 16), (4, 4)))
    lower_three = bell_draw(key_list[2], (POLES, 8, 3, W, W), (6 * W) ** -0.5, 0.078125, ((0, 4), (3, 16), (4, 4)))
    diag_inverse = draw_diag_inverse(jax.random.fold_in(key_list[9], 71), 0)
    pole_weight = jnp.clip(jnp.exp(math.log(3.0) - 2.3025851 * jax.random.uniform(key_list[4], (POLES,), jnp.float32) ** steps_of(key_list[4], (POLES,), ((0, 4),), -0.2, 0.2)), 0.3, 3.0)
    super_sizes = draw_super_sizes(jax.random.fold_in(key_list[9], 71), 0)
    parents = draw_parents(jax.random.fold_in(key_list[9], 71), 0)
    keep_two = plant((jax.random.randint(key_list[7], (4,), 0, 3) < 2).astype(jnp.int32), jax.random.fold_in(key_list[7], 1), 0, 1)
    keep_three = plant((jax.random.randint(key_list[8], (8, 2), 0, 3) < 2).astype(jnp.int32), jax.random.fold_in(key_list[8], 1), 0, 1)
    return {"lower_one": lower_one, "lower_two": lower_two, "lower_three": lower_three, "diag_inverse": diag_inverse, "pole_weight": pole_weight, "super_sizes": super_sizes, "parents": parents, "keep_two": keep_two, "keep_three": keep_three}


def live_table(super_sizes):
    places = jnp.arange(SUPB, dtype=jnp.int32)
    return (places[None, None, :] < super_sizes[:, :, None]).reshape(NODES, W).astype(jnp.bfloat16)


def descend(panels, factor, dinv_blocks):
    node_count = factor.shape[0]
    depth = factor.shape[1]
    columns = factor.reshape(node_count, depth * W, W).astype(jnp.float32)
    inverse = -jnp.einsum("xik,xkj->xij", panels.astype(jnp.float32), columns, precision=lax.Precision.HIGHEST)
    inverse = inverse.astype(jnp.bfloat16)
    product = jnp.einsum("xia,xij->xaj", inverse.astype(jnp.float32), columns, precision=lax.Precision.HIGHEST)
    diagonal = (dinv_blocks.astype(jnp.float32) - product).astype(jnp.bfloat16)
    return inverse, diagonal


def extend_paths(panels, inverse, diagonal):
    upper = jnp.concatenate([panels, inverse], axis=2)
    lower = jnp.concatenate([jnp.swapaxes(inverse, 1, 2), diagonal], axis=2)
    return jnp.concatenate([upper, lower], axis=1)


def split_blocks(inverse, diagonal):
    node_count = inverse.shape[0]
    depth = inverse.shape[1] // W
    return jnp.concatenate([inverse.reshape(node_count, depth, W, W), diagonal[:, None]], axis=1)


def one_pole(lower_one, lower_two, lower_three, dinv, live_mask, parent_two, parent_three, keep_two, keep_three):
    masked = dinv * live_mask[:, :, None] * live_mask[:, None, :]
    grand_parent = parent_two[parent_three]
    rows_one = jnp.broadcast_to(live_mask[0], (2, 1, W))
    factor_one = lower_one * rows_one[:, :, :, None] * live_mask[1:3][:, None, None, :]
    panels_one = jnp.broadcast_to(masked[0], (2, W, W))
    inverse_one, diagonal_one = descend(panels_one, factor_one, masked[1:3])
    paths_one = extend_paths(panels_one, inverse_one, diagonal_one)
    rows_two = jnp.stack([live_mask[0][None, :] * keep_two[:, None].astype(jnp.bfloat16), live_mask[1 + parent_two]], axis=1)
    factor_two = lower_two * rows_two[:, :, :, None] * live_mask[3:7][:, None, None, :]
    panels_two = paths_one[parent_two]
    inverse_two, diagonal_two = descend(panels_two, factor_two, masked[3:7])
    paths_two = extend_paths(panels_two, inverse_two, diagonal_two)
    rows_three = jnp.stack([live_mask[0][None, :] * keep_three[:, 0:1].astype(jnp.bfloat16), live_mask[1 + grand_parent] * keep_three[:, 1:2].astype(jnp.bfloat16), live_mask[3 + parent_three]], axis=1)
    factor_three = lower_three * rows_three[:, :, :, None] * live_mask[7:15][:, None, None, :]
    inverse_three, diagonal_three = descend(paths_two[parent_three], factor_three, masked[7:15])
    top_blocks = jnp.concatenate([masked[0:1], split_blocks(inverse_one, diagonal_one).reshape(4, W, W)], axis=0)
    return top_blocks, split_blocks(inverse_two, diagonal_two), split_blocks(inverse_three, diagonal_three)


def reference(lower_one, lower_two, lower_three, diag_inverse, pole_weight, super_sizes, parents, keep_two, keep_three):
    live_mask = live_table(super_sizes)
    parent_two = parents[0:4]
    parent_three = parents[4:12]

    def accumulate(running, pole_index):
        blocks = one_pole(lower_one[pole_index], lower_two[pole_index], lower_three[pole_index], diag_inverse[pole_index], live_mask, parent_two, parent_three, keep_two, keep_three)
        weight = pole_weight[pole_index]
        updated = (running[0] + weight * blocks[0].astype(jnp.float32), running[1] + weight * blocks[1].astype(jnp.float32), running[2] + weight * blocks[2].astype(jnp.float32))
        return updated, None

    initial = (jnp.zeros((5, W, W), jnp.float32), jnp.zeros((4, 3, W, W), jnp.float32), jnp.zeros((8, 4, W, W), jnp.float32))
    totals, unused = lax.scan(accumulate, initial, jnp.arange(POLES, dtype=jnp.int32))
    return (totals[0], totals[1], totals[2])
```

```python
import jax
import jax.numpy as jnp
from jax import lax
from jax.experimental import pallas as pl
from jax.experimental.pallas import tpu as pltpu
from jax.sharding import PartitionSpec as P

MESH = pl.DeviceIdType.MESH
F32 = jnp.float32
BF16 = jnp.bfloat16
SUPB = 512
W = 1024
ROWS = 64
COLS = 256
ZN = 8
YN = 4
XN = 4

L2A, L2B, L1, D0, D1, D2, L3A, L3B, L3C = range(9)
TWO_AT = 32
ONE_AT = 44


def positions(parents_ref):
    two = [parents_ref[i] for i in range(4)]
    three = [parents_ref[4 + k] for k in range(8)]
    place_two = []
    for i in range(4):
        before = sum([(two[h] == two[i]).astype(jnp.int32) for h in range(i)], jnp.int32(0))
        place_two.append(2 * two[i] + before)
    place_three = []
    for k in range(8):
        before = sum([(three[h] == three[k]).astype(jnp.int32) for h in range(k)], jnp.int32(0))
        above = sum([jnp.where(three[k] == i, place_two[i], 0) for i in range(4)], jnp.int32(0))
        place_three.append(2 * above + before)
    return place_two, place_three


def node_at(places, place):
    return sum([jnp.where(p == place, i, 0) for i, p in enumerate(places)], jnp.int32(0))


def limits(sizes_ref):
    row = lax.axis_index("row") * ROWS
    col = lax.axis_index("col") * COLS
    row_sup, row_at = row // SUPB, row % SUPB
    col_sup, col_at = col // SUPB, col % SUPB
    return (lambda n: sizes_ref[n, row_sup] - row_at), (lambda n: sizes_ref[n, col_sup] - col_at)


def masked(block, rows_live, cols_live):
    rows = lax.broadcasted_iota(jnp.int32, (ROWS, COLS), 0) < rows_live
    cols = lax.broadcasted_iota(jnp.int32, (ROWS, COLS), 1) < cols_live
    return jnp.where(rows & cols, block.astype(F32), 0.0)


def prepare(one_ref, two_ref, three_ref, diag_ref, sizes_ref, parents_ref, keep_two_ref, keep_three_ref, out_ref):
    place_two, place_three = positions(parents_ref)
    rows_of, cols_of = limits(sizes_ref)
    for z in range(ZN):
        i, j = z // 4, z // 2
        n2 = node_at(place_two, j)
        n3 = node_at(place_three, z)
        c0, c1, c2, c3 = cols_of(0), cols_of(1 + i), cols_of(3 + n2), cols_of(7 + n3)
        r0, r1, r2 = rows_of(0), rows_of(1 + i), rows_of(3 + n2)
        out_ref[z, L2A] = masked(two_ref[n2, 0], r0 * keep_two_ref[n2], c2).astype(BF16)
        out_ref[z, L2B] = masked(two_ref[n2, 1], r1, c2).astype(BF16)
        out_ref[z, L1] = masked(one_ref[i], r0, c1).astype(BF16)
        out_ref[z, D0] = masked(diag_ref[0], r0, c0).astype(BF16)
        out_ref[z, D1] = masked(diag_ref[1 + i], r1, c1).astype(BF16)
        out_ref[z, D2] = masked(diag_ref[3 + n2], r2, c2).astype(BF16)
        out_ref[z, L3A] = masked(three_ref[n3, 0], r0 * keep_three_ref[n3, 0], c3).astype(BF16)
        out_ref[z, L3B] = masked(three_ref[n3, 1], r1 * keep_three_ref[n3, 1], c3).astype(BF16)
        out_ref[z, L3C] = masked(three_ref[n3, 2], r2, c3).astype(BF16)


def dot(a, b):
    return jnp.dot(a, b, preferred_element_type=F32)


def tree(
    in_ref,
    out_ref,
    mat,
    res,
    yab,
    ybb,
    za,
    zb,
    zc,
    yat,
    ybt,
    yct,
    z_send,
    z_recv,
    y_send,
    y_recv,
    f_send,
    f_recv,
    d_send,
    d_recv,
    o_send,
    o_recv,
    own_sem,
):
    row, y = lax.axis_index("row"), lax.axis_index("col")
    z, core = row // 2, row % 2
    other = row + 1 - 2 * core
    up, down = (y + 1) % YN, (y + YN - 1) % YN
    far = (y + 2) % YN

    barrier = pltpu.get_barrier_semaphore()
    for d in range(1, 16):
        pl.semaphore_signal(barrier, inc=1, device_id={"row": (row + d) % 16}, device_id_type=MESH)
    for peer in (up, down):
        pl.semaphore_signal(barrier, inc=1, device_id={"col": peer}, device_id_type=MESH)
    pl.semaphore_wait(barrier, 17)

    def cols(at, width=COLS):
        return pl.ds(pl.multiple_of(at * width, width), width)

    def remote(src, dst, send, recv, **device):
        return pltpu.make_async_remote_copy(
            src_ref=src, dst_ref=dst, send_sem=send, recv_sem=recv, device_id=device, device_id_type=MESH
        )

    def along_z(g, d):
        to = (z + d) % ZN
        blocks = pl.ds(3 * g, 3)
        return remote(
            in_ref.at[to, blocks],
            mat.at[blocks, z, core, :, cols(y)],
            z_send.at[g, d - 1],
            z_recv.at[g, d - 1],
            row=2 * to + core,
        )

    def along_y(b, way, to):
        piece = mat.at[b, :, core, :, cols(y)]
        return remote(piece, piece, y_send.at[b, way], y_recv.at[b, way], col=to)

    def onward(b, way, source, to):
        piece = mat.at[b, pl.ds(4 * way, 4), core, :, cols(source)]
        return remote(piece, piece, f_send.at[b, way], f_recv.at[b, way], col=to)

    def across(b, n, source):
        piece = mat.at[b, :, core, :, cols(source)]
        return remote(piece, piece, d_send.at[b, n], d_recv.at[b, n], row=other)

    own = pltpu.make_async_copy(in_ref.at[z], mat.at[:, z, core, :, cols(y)], own_sem)
    own.start()
    for g in range(3):
        for d in range(1, ZN):
            along_z(g, d).start()
    own.wait()

    def spread(b, carry):
        along_y(b, 0, up).start()
        along_y(b, 1, down).start()
        across(b, 0, y).start()
        return carry

    def forward(b, carry):
        along_y(b, 0, up).wait_recv()
        onward(b, 0, down, up).start()
        across(b, 1, down).start()
        along_y(b, 1, down).wait_recv()
        onward(b, 1, up, down).start()
        across(b, 2, up).start()
        return carry

    def finish(b, carry):
        onward(b, 0, down, up).wait_recv()
        onward(b, 1, up, down).wait_recv()
        across(b, 3, far).start()
        return carry

    for g in range(3):
        for d in range(1, ZN):
            along_z(g, d).wait_recv()
        lax.fori_loop(3 * g, 3 * g + 3, spread, 0)
    lax.fori_loop(0, 9, forward, 0)
    lax.fori_loop(0, 9, finish, 0)

    def settle(b, carry):
        along_y(b, 0, up).wait_send()
        along_y(b, 1, down).wait_send()
        onward(b, 0, down, up).wait_send()
        onward(b, 1, up, down).wait_send()
        for n, source in enumerate((y, down, up, far)):
            across(b, n, source).wait()
        return carry

    lax.fori_loop(0, 9, settle, 0)
    for g in range(3):
        for d in range(1, ZN):
            along_z(g, d).wait_send()

    mine = 2 * y + core
    half = 2 * y + z % 2

    def tall(b, t):
        return mat[b, pl.ds(2 * t, 2)].reshape(256, W)

    def wide(b, t):
        return mat[b, :, :, :, cols(t)].reshape(W, 256)

    def strip(b, at):
        return mat[b, :, :, :, cols(at, 128)].reshape(W, 128)

    def strip_at(b, t, at):
        return mat[b, pl.ds(2 * t, 2), :, :, cols(at, 128)].reshape(256, 128)

    def rows_at(t):
        return pl.ds(pl.multiple_of(t * 256, 256), 256)

    def first(t, carry):
        low = strip(L3C, mine)
        at = rows_at(t)
        yab[at, 0:128] = strip_at(L3A, t, mine).astype(F32) - dot(tall(L2A, t), low)
        yab[at, 128:256] = strip_at(L2A, t, half).astype(F32)
        ybb[at, 0:128] = (strip_at(L3B, t, mine).astype(F32) - dot(tall(L2B, t), low)).astype(BF16)
        ybb[at, 128:256] = strip_at(L2B, t, half)
        return carry

    lax.fori_loop(0, 4, first, 0)

    def second(t, carry):
        at = rows_at(t)
        top = yab[at, :] - dot(tall(L1, t), ybb[...])
        yat[0:256, at] = top.T.astype(BF16)
        yat[256:384, at] = strip_at(L1, t, half).astype(F32).T.astype(BF16)
        ybt[:, at] = ybb[at, :].astype(F32).T.astype(BF16)
        yct[:, at] = strip_at(L3C, t, mine).astype(F32).T.astype(BF16)
        return carry

    lax.fori_loop(0, 4, second, 0)

    def put(n, t, value):
        res[n, pl.ds(4 * t, 4)] = value.T.astype(BF16).reshape(4, ROWS, 128)

    def root_rows(t, carry):
        value = dot(yat[...], wide(D0, t))
        za[:, rows_at(t)] = value.astype(BF16)
        put(0, t, -value[0:128])
        put(4, t, -value[128:256])
        put(7, t, -value[256:384])
        return carry

    lax.fori_loop(0, 4, root_rows, 0)

    def one_rows(t, carry):
        back = dot(za[...], wide(L1, t))
        value = dot(ybt[...], wide(D1, t)) - back[0:256]
        zb[:, rows_at(t)] = value.astype(BF16)
        put(1, t, -value[0:128])
        put(5, t, -value[128:256])
        put(8, t, back[256:384])
        return carry

    lax.fori_loop(0, 4, one_rows, 0)

    def two_rows(t, carry):
        back = dot(za[0:256, :], wide(L2A, t)) + dot(zb[...], wide(L2B, t))
        value = dot(yct[...], wide(D2, t)) - back[0:128]
        zc[:, rows_at(t)] = value.astype(BF16)
        put(2, t, -value)
        put(6, t, back[128:256])
        return carry

    lax.fori_loop(0, 4, two_rows, 0)

    def three_rows(t, carry):
        value = dot(za[0:128, :], wide(L3A, t)) + dot(zb[0:128, :], wide(L3B, t)) + dot(zc[...], wide(L3C, t))
        put(3, t, value)
        return carry

    lax.fori_loop(0, 4, three_rows, 0)

    def three_to(d):
        to = (row + d) % 16
        return remote(
            res.at[0:4, to],
            out_ref.at[pl.ds(4 * z, 4), :, cols(core, 128)],
            o_send.at[d - 1],
            o_recv.at[d - 1],
            row=to,
        )

    def two_to(d):
        to = (z + d) % ZN
        return remote(
            res.at[4:7, 2 * to + core],
            out_ref.at[pl.ds(TWO_AT + 3 * (z // 2), 3), :, cols(z % 2, 128)],
            o_send.at[14 + d],
            o_recv.at[14 + d],
            row=2 * to + core,
        )

    def one_to(n, d):
        to = (z + ZN - d) % ZN
        return remote(
            res.at[7:9, 2 * to + core],
            out_ref.at[pl.ds(ONE_AT + 2 * (z // 4), 2), :, cols(z % 2, 128)],
            o_send.at[22 + n],
            o_recv.at[22 + n],
            row=2 * to + core,
        )

    def keep(blocks, at, count, side):
        here = pltpu.make_async_copy(
            res.at[blocks, row], out_ref.at[pl.ds(at, count), :, cols(side, 128)], own_sem
        )
        here.start()
        here.wait()

    for d in range(1, 16):
        three_to(d).start()
    for d in range(1, ZN):
        two_to(d).start()
    for n, d in enumerate((1, 4, 5)):
        one_to(n, d).start()
    keep(slice(0, 4), 4 * z, 4, core)
    keep(slice(4, 7), TWO_AT + 3 * (z // 2), 3, z % 2)
    keep(slice(7, 9), ONE_AT + 2 * (z // 4), 2, z % 2)
    for d in range(1, 16):
        three_to(d).wait()
    for d in range(1, ZN):
        two_to(d).wait()
    for n, d in enumerate((1, 4, 5)):
        one_to(n, d).wait()


def poles(
    blocks_ref,
    diag_ref,
    sizes_ref,
    parents_ref,
    weight_ref,
    top_ref,
    two_ref,
    three_ref,
    mine,
    theirs,
    top,
    tops,
    weights,
    own_weight,
    send,
    recv,
):
    pole = lax.axis_index("pole")
    barrier = pltpu.get_barrier_semaphore()
    for d in range(1, XN):
        pl.semaphore_signal(barrier, inc=1, device_id={"pole": (pole + d) % XN}, device_id_type=MESH)

    place_two, place_three = positions(parents_ref)
    rows_of, cols_of = limits(sizes_ref)

    def diagonal(n):
        return masked(diag_ref[n], rows_of(n), cols_of(n))

    own_weight[...] = jnp.full((8, 128), weight_ref[0], F32)
    top[0] = diagonal(0).astype(BF16)
    for i in range(2):
        top[1 + 2 * i] = blocks_ref[ONE_AT + 2 * i]
        top[2 + 2 * i] = (diagonal(1 + i) + blocks_ref[ONE_AT + 2 * i + 1].astype(F32)).astype(BF16)
    for i in range(4):
        at = TWO_AT + 3 * place_two[i]
        mine[i, 8] = blocks_ref[at]
        mine[i, 9] = blocks_ref[at + 1]
        mine[i, 10] = (diagonal(3 + i) + blocks_ref[at + 2].astype(F32)).astype(BF16)
    for k in range(8):
        at = 4 * place_three[k]
        to, first = k // 2, 4 * (k % 2)
        for q in range(3):
            mine[to, first + q] = blocks_ref[at + q]
        mine[to, first + 3] = (diagonal(7 + k) + blocks_ref[at + 3].astype(F32)).astype(BF16)

    def copies(d):
        to = (pole + d) % XN
        pairs = ((mine.at[to], theirs.at[d - 1]), (top, tops.at[d - 1]), (own_weight, weights.at[d - 1]))
        return [
            pltpu.make_async_remote_copy(
                src_ref=src,
                dst_ref=dst,
                send_sem=send.at[d - 1, n],
                recv_sem=recv.at[d - 1, n],
                device_id={"pole": to},
                device_id_type=MESH,
            )
            for n, (src, dst) in enumerate(pairs)
        ]

    pl.semaphore_wait(barrier, XN - 1)
    for d in range(1, XN):
        for copy in copies(d):
            copy.start()
    for d in range(1, XN):
        for copy in copies(d):
            copy.wait()

    scale = [weight_ref[0]] + [weights[d, 0:1, 0:1] for d in range(XN - 1)]

    def total(own, others):
        value = scale[0] * own.astype(F32)
        for d in range(XN - 1):
            value = value + scale[d + 1] * others(d).astype(F32)
        return value

    for n in range(5):
        top_ref[n] = total(top[n], lambda d: tops[d, n])
    for n in range(3):
        two_ref[0, n] = total(mine[pole, 8 + n], lambda d: theirs[d, 8 + n])
    for n in range(8):
        three_ref[n // 4, n % 4] = total(mine[pole, n], lambda d: theirs[d, n])


VMEM = pl.BlockSpec(memory_space=pltpu.VMEM)
SMEM = pl.BlockSpec(memory_space=pltpu.SMEM)
ANY = pl.BlockSpec(memory_space=pl.ANY)
GRANT = 52 * 1024 * 1024


def local(
    lower_one,
    lower_two,
    lower_three,
    diag_inverse,
    pole_weight,
    super_sizes,
    parents,
    keep_two,
    keep_three,
):
    one = lower_one.reshape(2, ROWS, COLS)
    two = lower_two.reshape(4, 2, ROWS, COLS)
    three = lower_three.reshape(8, 3, ROWS, COLS)
    diag = diag_inverse.reshape(15, ROWS, COLS)

    packed = pl.pallas_call(
        prepare,
        out_shape=jax.ShapeDtypeStruct((ZN, 9, ROWS, COLS), BF16),
        in_specs=[VMEM] * 4 + [SMEM] * 4,
        out_specs=VMEM,
        compiler_params=pltpu.CompilerParams(vmem_limit_bytes=GRANT),
    )(one, two, three, diag, super_sizes, parents, keep_two, keep_three)

    dma = pltpu.SemaphoreType.DMA
    blocks = pl.pallas_call(
        tree,
        out_shape=jax.ShapeDtypeStruct((48, ROWS, COLS), BF16),
        in_specs=[ANY],
        out_specs=ANY,
        scratch_shapes=[
            pltpu.VMEM((9, ZN, 2, ROWS, W), BF16),
            pltpu.VMEM((9, 16, ROWS, 128), BF16),
            pltpu.VMEM((W, 256), F32),
            pltpu.VMEM((W, 256), BF16),
            pltpu.VMEM((384, W), BF16),
            pltpu.VMEM((256, W), BF16),
            pltpu.VMEM((128, W), BF16),
            pltpu.VMEM((384, W), BF16),
            pltpu.VMEM((256, W), BF16),
            pltpu.VMEM((128, W), BF16),
            dma((3, 7)),
            dma((3, 7)),
            dma((9, 2)),
            dma((9, 2)),
            dma((9, 2)),
            dma((9, 2)),
            dma((9, 4)),
            dma((9, 4)),
            dma((25,)),
            dma((25,)),
            dma,
        ],
        compiler_params=pltpu.CompilerParams(
            collective_id=0, has_side_effects=True, vmem_limit_bytes=GRANT
        ),
    )(packed)

    return pl.pallas_call(
        poles,
        out_shape=(
            jax.ShapeDtypeStruct((5, ROWS, COLS), F32),
            jax.ShapeDtypeStruct((1, 3, ROWS, COLS), F32),
            jax.ShapeDtypeStruct((2, 4, ROWS, COLS), F32),
        ),
        in_specs=[VMEM, VMEM, SMEM, SMEM, SMEM],
        out_specs=(VMEM, VMEM, VMEM),
        scratch_shapes=[
            pltpu.VMEM((XN, 11, ROWS, COLS), BF16),
            pltpu.VMEM((XN - 1, 11, ROWS, COLS), BF16),
            pltpu.VMEM((5, ROWS, COLS), BF16),
            pltpu.VMEM((XN - 1, 5, ROWS, COLS), BF16),
            pltpu.VMEM((XN - 1, 8, 128), F32),
            pltpu.VMEM((8, 128), F32),
            dma((XN - 1, 3)),
            dma((XN - 1, 3)),
        ],
        compiler_params=pltpu.CompilerParams(
            collective_id=1, has_side_effects=True, vmem_limit_bytes=GRANT
        ),
    )(blocks, diag, super_sizes, parents, pole_weight)


def solution(mesh):
    placed = (
        P("pole", None, None, "row", "col"),
        P("pole", None, None, "row", "col"),
        P("pole", None, None, "row", "col"),
        P("pole", None, "row", "col"),
        P("pole"),
        P(),
        P(),
        P(),
        P(),
    )
    return jax.shard_map(
        local,
        mesh=mesh,
        in_specs=placed,
        out_specs=(
            P(None, "row", "col"),
            P("pole", None, "row", "col"),
            P("pole", None, "row", "col"),
        ),
        check_vma=False,
    )
```

```python
import jax
import jax.numpy as jnp
from jax import lax
from jax.experimental import pallas as pl
from jax.experimental.pallas import tpu as pltpu
from jax.sharding import PartitionSpec as P

MESH = pl.DeviceIdType.MESH
F32 = jnp.float32
BF16 = jnp.bfloat16
SUPB = 512
W = 1024
ROWS = 64
COLS = 256
ZN = 8
YN = 4
XN = 4

L2A, L2B, L1, D0, D1, D2, L3A, L3B, L3C = range(9)


def positions(parents_ref):
    two = [parents_ref[i] for i in range(4)]
    three = [parents_ref[4 + k] for k in range(8)]
    place_two = []
    for i in range(4):
        before = sum([(two[h] == two[i]).astype(jnp.int32) for h in range(i)], jnp.int32(0))
        place_two.append(2 * two[i] + before)
    place_three = []
    for k in range(8):
        before = sum([(three[h] == three[k]).astype(jnp.int32) for h in range(k)], jnp.int32(0))
        above = sum([jnp.where(three[k] == i, place_two[i], 0) for i in range(4)], jnp.int32(0))
        place_three.append(2 * above + before)
    return place_two, place_three


def node_at(places, place):
    return sum([jnp.where(p == place, i, 0) for i, p in enumerate(places)], jnp.int32(0))


def limits(sizes_ref):
    row = lax.axis_index("row") * ROWS
    col = lax.axis_index("col") * COLS
    row_sup, row_at = row // SUPB, row % SUPB
    col_sup, col_at = col // SUPB, col % SUPB
    return (lambda n: sizes_ref[n, row_sup] - row_at), (lambda n: sizes_ref[n, col_sup] - col_at)


def masked(block, rows_live, cols_live):
    rows = lax.broadcasted_iota(jnp.int32, (ROWS, COLS), 0) < rows_live
    cols = lax.broadcasted_iota(jnp.int32, (ROWS, COLS), 1) < cols_live
    return jnp.where(rows & cols, block.astype(F32), 0.0)


def dot(a, b):
    return jnp.dot(a, b, preferred_element_type=F32)


BATCHES = (((0, 2), (4, 6), (7, 9)), ((2, 3), (6, 7), None), ((3, 4), None, None))


def tree(
    one_hbm,
    two_hbm,
    three_hbm,
    diag_hbm,
    sizes_ref,
    parents_ref,
    keep_two_ref,
    keep_three_ref,
    weight_ref,
    top_ref,
    out_two_ref,
    out_three_ref,
    one_ref,
    two_ref,
    three_ref,
    diag_ref,
    in_ref,
    mat,
    res,
    yab,
    ybb,
    za,
    zb,
    zc,
    yat,
    ybt,
    yct,
    got_a,
    got_b,
    got_c,
    mine_x,
    theirs,
    top,
    tops,
    weights,
    own_weight,
    load_sem,
    z_send,
    z_recv,
    y_send,
    y_recv,
    f_send,
    f_recv,
    d_send,
    d_recv,
    o_send,
    o_recv,
    keep_sem,
    x_send,
    x_recv,
    own_sem,
):
    pole, row, y = lax.axis_index("pole"), lax.axis_index("row"), lax.axis_index("col")
    z, core = row // 2, row % 2
    other = row + 1 - 2 * core
    up, down = (y + 1) % YN, (y + YN - 1) % YN
    far = (y + 2) % YN

    barrier = pltpu.get_barrier_semaphore()
    for d in range(1, 16):
        pl.semaphore_signal(barrier, inc=1, device_id={"row": (row + d) % 16}, device_id_type=MESH)
    for peer in (up, down):
        pl.semaphore_signal(barrier, inc=1, device_id={"col": peer}, device_id_type=MESH)
    for d in range(1, XN):
        pl.semaphore_signal(barrier, inc=1, device_id={"pole": (pole + d) % XN}, device_id_type=MESH)

    loads = [
        pltpu.make_async_copy(src, dst, load_sem.at[n])
        for n, (src, dst) in enumerate(
            ((two_hbm, two_ref), (one_hbm, one_ref), (diag_hbm, diag_ref), (three_hbm, three_ref))
        )
    ]
    for load in loads:
        load.start()

    place_two, place_three = positions(parents_ref)
    rows_of, cols_of = limits(sizes_ref)
    order_two = [node_at(place_two, j) for j in range(4)]
    order_three = [node_at(place_three, k) for k in range(8)]
    r0, c0 = rows_of(0), cols_of(0)
    r1, c1 = [rows_of(1 + i) for i in range(2)], [cols_of(1 + i) for i in range(2)]
    r2, c2 = [rows_of(3 + n) for n in order_two], [cols_of(3 + n) for n in order_two]
    c3 = [cols_of(7 + n) for n in order_three]
    load_of = {L2A: 0, L2B: 0, L1: 1, D0: 2, D1: 2, D2: 2, L3A: 3, L3B: 3, L3C: 3}

    def block(b, to):
        i, j = to // 4, to // 2
        n2, n3 = order_two[j], order_three[to]
        if b == L2A:
            return masked(two_ref[n2, 0], r0 * keep_two_ref[n2], c2[j])
        if b == L2B:
            return masked(two_ref[n2, 1], r1[i], c2[j])
        if b == L1:
            return masked(one_ref[i], r0, c1[i])
        if b == D0:
            return masked(diag_ref[0], r0, c0)
        if b == D1:
            return masked(diag_ref[1 + i], r1[i], c1[i])
        if b == D2:
            return masked(diag_ref[3 + n2], r2[j], c2[j])
        if b == L3A:
            return masked(three_ref[n3, 0], r0 * keep_three_ref[n3, 0], c3[to])
        if b == L3B:
            return masked(three_ref[n3, 1], r1[i] * keep_three_ref[n3, 1], c3[to])
        return masked(three_ref[n3, 2], r2[j], c3[to])

    def cols(at, width=COLS):
        return pl.ds(pl.multiple_of(at * width, width), width)

    def remote(src, dst, send, recv, **device):
        return pltpu.make_async_remote_copy(
            src_ref=src, dst_ref=dst, send_sem=send, recv_sem=recv, device_id=device, device_id_type=MESH
        )

    def along_z(b, d):
        to = (z + d) % ZN
        return remote(
            in_ref.at[to, b],
            mat.at[b, z, core, :, cols(y)],
            z_send.at[b, d - 1],
            z_recv.at[b, d - 1],
            row=2 * to + core,
        )

    def own_copy(b):
        return pltpu.make_async_copy(in_ref.at[z, b], mat.at[b, z, core, :, cols(y)], own_sem.at[b])

    def along_y(b, way, to):
        piece = mat.at[b, :, core, :, cols(y)]
        return remote(piece, piece, y_send.at[b, way], y_recv.at[b, way], col=to)

    def onward(b, way, source, to):
        piece = mat.at[b, pl.ds(4 * way, 4), core, :, cols(source)]
        return remote(piece, piece, f_send.at[b, way], f_recv.at[b, way], col=to)

    def across(b, n):
        piece = mat.at[b, :, core, :, cols((y, down, up, far)[n])]
        return remote(piece, piece, d_send.at[b, n], d_recv.at[b, n], row=other)

    loaded = set()

    def mask(b):
        if load_of[b] not in loaded:
            loaded.add(load_of[b])
            loads[load_of[b]].wait()
        for to in range(ZN):
            in_ref[to, b] = block(b, to).astype(BF16)

    def z_start(b):
        own_copy(b).start()
        for d in (4, 3, 5, 2, 6, 1, 7):
            along_z(b, d).start()

    def z_sent(b):
        for d in range(1, ZN):
            along_z(b, d).wait_send()

    def gathered(b):
        own_copy(b).wait()
        for d in range(1, ZN):
            along_z(b, d).wait_recv()
        across(b, 0).start()

    def spread(b):
        along_y(b, 0, up).start()
        along_y(b, 1, down).start()

    def forward(b):
        along_y(b, 0, up).wait_recv()
        onward(b, 0, down, up).start()
        along_y(b, 1, down).wait_recv()
        onward(b, 1, up, down).start()
        across(b, 1).start()
        across(b, 2).start()

    def finish(b):
        onward(b, 0, down, up).wait_recv()
        onward(b, 1, up, down).wait_recv()
        across(b, 3).start()

    def shared(b, first=0):
        for n in range(first, 4):
            across(b, n).wait_recv()

    mine = 2 * y + core
    half = 2 * y + z % 2

    def tall(b, t):
        return mat[b, pl.ds(2 * t, 2)].reshape(256, W)

    def wide(b, t):
        return mat[b, :, :, :, cols(t)].reshape(W, 256)

    def strip(b, at):
        return mat[b, :, :, :, cols(at, 128)].reshape(W, 128)

    def strip_at(b, t, at):
        return mat[b, pl.ds(2 * t, 2), :, :, cols(at, 128)].reshape(256, 128)

    def rows_at(t):
        return pl.ds(pl.multiple_of(t * 256, 256), 256)

    def first(t, carry):
        low = strip(L3C, mine)
        at = rows_at(t)
        yab[at, 0:128] = strip_at(L3A, t, mine).astype(F32) - dot(tall(L2A, t), low)
        yab[at, 128:256] = strip_at(L2A, t, half).astype(F32)
        ybb[at, 0:128] = (strip_at(L3B, t, mine).astype(F32) - dot(tall(L2B, t), low)).astype(BF16)
        ybb[at, 128:256] = strip_at(L2B, t, half)
        return carry

    def second(t, carry):
        at = rows_at(t)
        top = yab[at, :] - dot(tall(L1, t), ybb[...])
        yat[0:256, at] = top.T.astype(BF16)
        yat[256:384, at] = strip_at(L1, t, half).astype(F32).T.astype(BF16)
        ybt[:, at] = ybb[at, :].astype(F32).T.astype(BF16)
        yct[:, at] = strip_at(L3C, t, mine).astype(F32).T.astype(BF16)
        return carry

    def put(n, t, value):
        res[n, pl.ds(4 * t, 4)] = value.T.astype(BF16).reshape(4, ROWS, 128)

    def root_rows(t, carry):
        value = dot(yat[...], wide(D0, t))
        za[:, rows_at(t)] = value.astype(BF16)
        put(0, t, -value[0:128])
        put(4, t, -value[128:256])
        put(7, t, -value[256:384])
        return carry

    def one_rows(t, carry):
        back = dot(za[...], wide(L1, t))
        value = dot(ybt[...], wide(D1, t)) - back[0:256]
        zb[:, rows_at(t)] = value.astype(BF16)
        put(1, t, -value[0:128])
        put(5, t, -value[128:256])
        put(8, t, back[256:384])
        return carry

    def two_rows(t, carry):
        back = dot(za[0:256, :], wide(L2A, t)) + dot(zb[...], wide(L2B, t))
        value = dot(yct[...], wide(D2, t)) - back[0:128]
        zc[:, rows_at(t)] = value.astype(BF16)
        put(2, t, -value)
        put(6, t, back[128:256])
        return carry

    def three_rows(t, carry):
        value = dot(za[0:128, :], wide(L3A, t)) + dot(zb[0:128, :], wide(L3B, t)) + dot(zc[...], wide(L3C, t))
        put(3, t, value)
        return carry

    gots = (got_a, got_b, got_c)
    one_offsets = (1, 4, 5)

    def batch_copies(n):
        got = gots[n]
        three, two, one = BATCHES[n]
        count = three[1] - three[0]
        copies = []
        for d in range(1, 16):
            to = (row + d) % 16
            copies.append((res.at[three[0] : three[1], to], got.at[pl.ds(z * count, count), :, cols(core, 128)], to))
        if two is not None:
            at = ZN * count + (z // 2) * count
            for d in range(1, ZN):
                to = 2 * ((z + d) % ZN) + core
                copies.append((res.at[two[0] : two[1], to], got.at[pl.ds(at, count), :, cols(z % 2, 128)], to))
        if one is not None:
            at = (ZN + 4) * count + (z // 4) * count
            for d in one_offsets:
                to = 2 * ((z + ZN - d) % ZN) + core
                copies.append((res.at[one[0] : one[1], to], got.at[pl.ds(at, count), :, cols(z % 2, 128)], to))
        return [
            remote(src, dst, o_send.at[n, k], o_recv.at[n, k], row=to) for k, (src, dst, to) in enumerate(copies)
        ]

    def batch_kept(n):
        got = gots[n]
        three, two, one = BATCHES[n]
        count = three[1] - three[0]
        copies = [(three, z * count, core)]
        if two is not None:
            copies.append((two, (ZN + z // 2) * count, z % 2))
        if one is not None:
            copies.append((one, (ZN + 4 + z // 4) * count, z % 2))
        return [
            pltpu.make_async_copy(
                res.at[blocks[0] : blocks[1], row],
                got.at[pl.ds(at, count), :, cols(side, 128)],
                keep_sem.at[n, k],
            )
            for k, (blocks, at, side) in enumerate(copies)
        ]

    def leave(n):
        for copy in batch_copies(n) + batch_kept(n):
            copy.start()

    def landed(n):
        for copy in batch_kept(n):
            copy.wait()
        for copy in batch_copies(n):
            copy.wait_recv()

    def diagonal(n):
        return masked(diag_ref[n], rows_of(n), cols_of(n))

    X_BATCHES = ((0, 6), (6, 9), (9, 11))

    def pole_copies(n):
        copies = []
        for d in range(1, XN):
            to = (pole + d) % XN
            blocks = slice(*X_BATCHES[n])
            pairs = [(mine_x.at[to, blocks], theirs.at[d - 1, blocks])]
            if n == 0:
                pairs += [(top, tops.at[d - 1]), (own_weight, weights.at[d - 1])]
            for k, (src, dst) in enumerate(pairs):
                copies.append(remote(src, dst, x_send.at[n, d - 1, k], x_recv.at[n, d - 1, k], pole=to))
        return copies

    def order_a():
        own_weight[...] = jnp.full((8, 128), weight_ref[0], F32)
        top[0] = diagonal(0).astype(BF16)
        for i in range(2):
            top[1 + 2 * i] = got_a[24 + 2 * i]
            top[2 + 2 * i] = (diagonal(1 + i) + got_a[25 + 2 * i].astype(F32)).astype(BF16)
        for i in range(4):
            mine_x[i, 4] = got_a[16 + 2 * place_two[i]]
            mine_x[i, 5] = got_a[17 + 2 * place_two[i]]
        for k in range(8):
            at = 2 * (k % 2)
            mine_x[k // 2, at] = got_a[2 * place_three[k]]
            mine_x[k // 2, at + 1] = got_a[2 * place_three[k] + 1]

    def order_b():
        for i in range(4):
            mine_x[i, 8] = (diagonal(3 + i) + got_b[8 + place_two[i]].astype(F32)).astype(BF16)
        for k in range(8):
            mine_x[k // 2, 6 + k % 2] = got_b[place_three[k]]

    def order_c():
        for k in range(8):
            mine_x[k // 2, 9 + k % 2] = (diagonal(7 + k) + got_c[place_three[k]].astype(F32)).astype(BF16)

    def to_poles(n):
        for copy in pole_copies(n):
            copy.start()

    def from_poles(n):
        for copy in pole_copies(n):
            copy.wait_recv()

    def total(own, others):
        value = weight_ref[0] * own.astype(F32)
        for d in range(XN - 1):
            value = value + weights[d, 0:1, 0:1] * others(d).astype(F32)
        return value

    def summed(n):
        return total(mine_x[pole, n], lambda d: theirs[d, n])

    def stage(body):
        lax.fori_loop(0, 4, body, 0)

    mask(0)
    pl.semaphore_wait(barrier, 15 + 2 + 3)
    z_start(0)
    for b in range(1, 9):
        mask(b)
    z_sent(0)
    z_start(1)
    gathered(0)
    spread(0)
    z_sent(1)
    z_start(2)
    gathered(1)
    spread(1)
    z_sent(2)
    z_start(3)
    gathered(2)
    forward(0)
    spread(2)
    z_sent(3)
    z_start(4)
    gathered(3)
    forward(1)
    spread(3)
    finish(0)
    z_sent(4)
    z_start(5)
    gathered(4)
    z_sent(5)
    z_start(6)
    forward(2)
    spread(4)
    finish(1)
    gathered(5)
    z_sent(6)
    z_start(7)
    gathered(6)
    forward(3)
    spread(5)
    finish(2)
    z_sent(7)
    z_start(8)
    gathered(7)
    shared(0)
    shared(1)
    forward(4)
    spread(6)
    finish(3)
    gathered(8)
    for b in (6, 7, 8):
        across(b, 0).wait_recv()
    stage(first)
    shared(2)
    stage(second)
    forward(5)
    spread(7)
    finish(4)
    shared(3)
    stage(root_rows)
    shared(4)
    stage(one_rows)
    leave(0)
    forward(6)
    spread(8)
    finish(5)
    shared(5)
    stage(two_rows)
    leave(1)
    forward(7)
    finish(6)
    landed(0)
    order_a()
    to_poles(0)
    forward(8)
    finish(7)
    landed(1)
    order_b()
    to_poles(1)
    finish(8)
    for b in (6, 7, 8):
        shared(b, 1)
    stage(three_rows)
    leave(2)
    from_poles(0)
    for n in range(5):
        top_ref[n] = total(top[n], lambda d: tops[d, n])
    for n in range(2):
        out_two_ref[0, n] = summed(4 + n)
    for n in range(4):
        out_three_ref[n // 2, n % 2] = summed(n)
    landed(2)
    order_c()
    to_poles(2)
    from_poles(1)
    out_two_ref[0, 2] = summed(8)
    for n in range(2):
        out_three_ref[n, 2] = summed(6 + n)
    from_poles(2)
    for n in range(2):
        out_three_ref[n, 3] = summed(9 + n)

    z_sent(8)
    for b in range(9):
        along_y(b, 0, up).wait_send()
        along_y(b, 1, down).wait_send()
        onward(b, 0, down, up).wait_send()
        onward(b, 1, up, down).wait_send()
        for n in range(4):
            across(b, n).wait_send()
    for n in range(3):
        for copy in batch_copies(n) + pole_copies(n):
            copy.wait_send()


VMEM = pl.BlockSpec(memory_space=pltpu.VMEM)
SMEM = pl.BlockSpec(memory_space=pltpu.SMEM)
ANY = pl.BlockSpec(memory_space=pl.ANY)
GRANT = 52 * 1024 * 1024


def local(
    lower_one,
    lower_two,
    lower_three,
    diag_inverse,
    pole_weight,
    super_sizes,
    parents,
    keep_two,
    keep_three,
):
    one = lower_one.reshape(2, ROWS, COLS)
    two = lower_two.reshape(4, 2, ROWS, COLS)
    three = lower_three.reshape(8, 3, ROWS, COLS)
    diag = diag_inverse.reshape(15, ROWS, COLS)

    dma = pltpu.SemaphoreType.DMA
    return pl.pallas_call(
        tree,
        out_shape=(
            jax.ShapeDtypeStruct((5, ROWS, COLS), F32),
            jax.ShapeDtypeStruct((1, 3, ROWS, COLS), F32),
            jax.ShapeDtypeStruct((2, 4, ROWS, COLS), F32),
        ),
        in_specs=[ANY] * 4 + [SMEM] * 5,
        out_specs=(VMEM, VMEM, VMEM),
        scratch_shapes=[
            pltpu.VMEM((2, ROWS, COLS), BF16),
            pltpu.VMEM((4, 2, ROWS, COLS), BF16),
            pltpu.VMEM((8, 3, ROWS, COLS), BF16),
            pltpu.VMEM((15, ROWS, COLS), BF16),
            pltpu.VMEM((ZN, 9, ROWS, COLS), BF16),
            pltpu.VMEM((9, ZN, 2, ROWS, W), BF16),
            pltpu.VMEM((9, 16, ROWS, 128), BF16),
            pltpu.VMEM((W, 256), F32),
            pltpu.VMEM((W, 256), BF16),
            pltpu.VMEM((384, W), BF16),
            pltpu.VMEM((256, W), BF16),
            pltpu.VMEM((128, W), BF16),
            pltpu.VMEM((384, W), BF16),
            pltpu.VMEM((256, W), BF16),
            pltpu.VMEM((128, W), BF16),
            pltpu.VMEM((28, ROWS, COLS), BF16),
            pltpu.VMEM((12, ROWS, COLS), BF16),
            pltpu.VMEM((8, ROWS, COLS), BF16),
            pltpu.VMEM((XN, 11, ROWS, COLS), BF16),
            pltpu.VMEM((XN - 1, 11, ROWS, COLS), BF16),
            pltpu.VMEM((5, ROWS, COLS), BF16),
            pltpu.VMEM((XN - 1, 5, ROWS, COLS), BF16),
            pltpu.VMEM((XN - 1, 8, 128), F32),
            pltpu.VMEM((8, 128), F32),
            dma((4,)),
            dma((9, 7)),
            dma((9, 7)),
            dma((9, 2)),
            dma((9, 2)),
            dma((9, 2)),
            dma((9, 2)),
            dma((9, 4)),
            dma((9, 4)),
            dma((3, 25)),
            dma((3, 25)),
            dma((3, 3)),
            dma((3, XN - 1, 3)),
            dma((3, XN - 1, 3)),
            dma((9,)),
        ],
        compiler_params=pltpu.CompilerParams(
            collective_id=0, has_side_effects=True, vmem_limit_bytes=GRANT
        ),
    )(one, two, three, diag, super_sizes, parents, keep_two, keep_three, pole_weight)


def solution(mesh):
    placed = (
        P("pole", None, None, "row", "col"),
        P("pole", None, None, "row", "col"),
        P("pole", None, None, "row", "col"),
        P("pole", None, "row", "col"),
        P("pole"),
        P(),
        P(),
        P(),
        P(),
    )
    return jax.shard_map(
        local,
        mesh=mesh,
        in_specs=placed,
        out_specs=(
            P(None, "row", "col"),
            P("pole", None, "row", "col"),
            P("pole", None, "row", "col"),
        ),
        check_vma=False,
    )
```

```python
import jax
import jax.numpy as jnp
from jax import lax
from jax.experimental import pallas as pl
from jax.experimental.pallas import tpu as pltpu
from jax.sharding import PartitionSpec as P

MESH = pl.DeviceIdType.MESH
F32 = jnp.float32
BF16 = jnp.bfloat16
SUPB = 512
W = 1024
ROWS = 64
COLS = 256
ZN = 8
YN = 4
XN = 4

L2A, L2B, L1, D0, D1, D2, L3A, L3B, L3C = range(9)


def mod(a, n):
    return a % n if isinstance(a, int) else lax.rem(a, n)


def div(a, n):
    return a // n if isinstance(a, int) else lax.div(a, n)


def positions(parents_ref):
    two = [parents_ref[i] for i in range(4)]
    three = [parents_ref[4 + k] for k in range(8)]
    place_two = []
    for i in range(4):
        before = sum([(two[h] == two[i]).astype(jnp.int32) for h in range(i)], jnp.int32(0))
        place_two.append(2 * two[i] + before)
    place_three = []
    for k in range(8):
        before = sum([(three[h] == three[k]).astype(jnp.int32) for h in range(k)], jnp.int32(0))
        above = sum([jnp.where(three[k] == i, place_two[i], 0) for i in range(4)], jnp.int32(0))
        place_three.append(2 * above + before)
    return place_two, place_three


def node_at(places, place):
    return sum([jnp.where(p == place, i, 0) for i, p in enumerate(places)], jnp.int32(0))


def limits(sizes_ref):
    row = lax.axis_index("row") * ROWS
    col = lax.axis_index("col") * COLS
    row_sup, row_at = div(row, SUPB), mod(row, SUPB)
    col_sup, col_at = div(col, SUPB), mod(col, SUPB)
    return (lambda n: sizes_ref[row_sup, n] - row_at), (lambda n: sizes_ref[col_sup, n] - col_at)


def below(limit, axis):
    places = lax.broadcasted_iota(jnp.int32, (ROWS, COLS), axis)
    return jnp.where(places < limit, 1.0, 0.0).astype(BF16)


def dot(a, b):
    return jnp.dot(a, b, preferred_element_type=F32)


X3A, X2A, X1, X3B, X2B, P1, X3C, P2, P3 = range(9)
BATCHES = 4
SHARE = {L2A: 2, L2B: 2, L1: 4, D0: 8, D1: 4, D2: 2, L3A: 1, L3B: 1, L3C: 1}
PART = ROWS // XN


def tree(
    one_hbm,
    two_hbm,
    three_hbm,
    diag_hbm,
    sizes_ref,
    parents_ref,
    keep_two_ref,
    keep_three_ref,
    weight_ref,
    top_ref,
    out_two_ref,
    out_three_ref,
    one_ref,
    two_ref,
    three_ref,
    diag_ref,
    in_ref,
    mat,
    res,
    yab,
    ybb,
    za,
    zb,
    zc,
    yat,
    ybt,
    yct,
    got_a,
    got_b,
    got_c,
    got_d,
    terms,
    sums,
    diag_mine,
    diag_theirs,
    diag_sum,
    mine_two,
    mine_three,
    mine_top,
    weights,
    own_weight,
    load_sem,
    z_send,
    z_recv,
    y_send,
    y_recv,
    f_recv,
    d_send,
    d_recv,
    s_recv,
    o_send,
    o_recv,
    x_send,
    x_recv,
    p_send,
    p_recv,
    g_send,
    g_recv,
):
    pole, row, y = lax.axis_index("pole"), lax.axis_index("row"), lax.axis_index("col")
    z, core = div(row, 2), mod(row, 2)
    other = row + 1 - 2 * core
    up, down = mod((y + 1), YN), mod((y + YN - 1), YN)
    far = mod((y + 2), YN)

    loads = [
        pltpu.make_async_copy(src, dst, load_sem.at[n])
        for n, (src, dst) in enumerate(
            ((two_hbm, two_ref), (one_hbm, one_ref), (diag_hbm, diag_ref), (three_hbm, three_ref))
        )
    ]
    for load in loads:
        load.start()

    barrier = pltpu.get_barrier_semaphore()
    for d in range(1, 16):
        pl.semaphore_signal(barrier, inc=1, device_id={"row": mod((row + d), 16)}, device_id_type=MESH)
    for peer in (up, down):
        pl.semaphore_signal(barrier, inc=1, device_id={"col": peer}, device_id_type=MESH)
    for d in range(1, XN):
        pl.semaphore_signal(barrier, inc=1, device_id={"pole": mod((pole + d), XN)}, device_id_type=MESH)

    place_two, place_three = positions(parents_ref)
    rows_of, cols_of = limits(sizes_ref)
    order_two = [node_at(place_two, j) for j in range(4)]
    order_three = [node_at(place_three, k) for k in range(8)]
    r0, c0 = rows_of(0), cols_of(0)
    r1, c1 = [rows_of(1 + i) for i in range(2)], [cols_of(1 + i) for i in range(2)]
    r2, c2 = [rows_of(3 + n) for n in order_two], [cols_of(3 + n) for n in order_two]
    c3 = [cols_of(7 + n) for n in order_three]
    load_of = {L2A: 0, L2B: 0, L1: 1, D0: 2, D1: 2, D2: 2, L3A: 3, L3B: 3, L3C: 3}

    def block(b, to):
        i, j = div(to, 4), div(to, 2)
        n2, n3 = order_two[j], order_three[to]
        if b == L2A:
            return two_ref[n2, 0] * rows[0] * below(c2[j] * keep_two_ref[n2], 1)
        if b == L2B:
            return two_ref[n2, 1] * rows[1 + i] * below(c2[j], 1)
        if b == L1:
            return one_ref[i] * rows[0] * below(c1[i], 1)
        if b == D0:
            return diag_ref[0] * rows[0] * below(c0, 1)
        if b == D1:
            return diag_ref[1 + i] * rows[1 + i] * below(c1[i], 1)
        if b == D2:
            return diag_ref[3 + n2] * rows[3 + j] * below(c2[j], 1)
        if b == L3A:
            return three_ref[n3, 0] * rows[0] * below(c3[to] * keep_three_ref[0, n3], 1)
        if b == L3B:
            return three_ref[n3, 1] * rows[1 + i] * below(c3[to] * keep_three_ref[1, n3], 1)
        return three_ref[n3, 2] * rows[3 + j] * below(c3[to], 1)

    rows, loaded = {}, set()

    def mask(b):
        if load_of[b] not in loaded:
            loaded.add(load_of[b])
            loads[load_of[b]].wait()
        for n in {L2B: (1, 2), D1: (1, 2), D2: (3, 4, 5, 6), L3B: (1, 2), L3C: (3, 4, 5, 6)}.get(b, (0,)):
            if n not in rows:
                rows[n] = below(r0 if n == 0 else r1[n - 1] if n < 3 else r2[n - 3], 0)
        for to in range(0, ZN, SHARE[b]):
            in_ref[to, b] = block(b, to)

    def cols(at, width=COLS):
        return pl.ds(pl.multiple_of(at * width, width), width)

    def remote(src, dst, send, recv, **device):
        return pltpu.make_async_remote_copy(
            src_ref=src, dst_ref=dst, send_sem=send, recv_sem=recv, device_id=device, device_id_type=MESH
        )

    def along_z(b, d):
        to = mod((z + d), ZN)
        return remote(
            in_ref.at[div(to, SHARE[b]) * SHARE[b], b],
            mat.at[b, z, core, :, cols(y)],
            z_send.at[b],
            z_recv.at[b],
            row=2 * to + core,
        )

    def own_copy(b):
        return pltpu.make_async_copy(
            in_ref.at[div(z, SHARE[b]) * SHARE[b], b], mat.at[b, z, core, :, cols(y)], z_recv.at[b]
        )

    def along_y(b, way, to):
        piece = mat.at[b, :, core, :, cols(y)]
        return remote(piece, piece, y_send.at[b], y_recv.at[b, way], col=to)

    def onward(b, way, source, to):
        piece = mat.at[b, pl.ds(4 * way, 4), core, :, cols(source)]
        return remote(piece, piece, y_send.at[b], f_recv.at[b, way], col=to)

    def across(b, n):
        piece = mat.at[b, :, core, :, cols((y, down, up, far)[n])]
        return remote(piece, piece, d_send.at[b], d_recv.at[b, min(n, 1)], row=other)

    def z_start(b):
        own_copy(b).start()
        for d in (4, 3, 5, 2, 6, 1, 7):
            along_z(b, d).start()

    def arrived(ref, sem):
        pltpu.make_async_copy(ref, ref, sem).wait()

    def z_sent(b):
        arrived(mat.at[b, 0 : ZN - 1, core, :, cols(y)], z_send.at[b])

    def gathered(b):
        arrived(mat.at[b, :, core, :, cols(y)], z_recv.at[b])
        across(b, 0).start()

    PIECES = ((1, 1), (2, 1), (3, 3), (2, 3), (1, 3), (2, 2))

    def piece_at(b, i, j):
        return mat.at[b, pl.ds(2 * (mod((y + YN + i), YN)), 2), core, :, cols(mod((y + YN + j), YN))]

    def piece_copy(b, n):
        i, j = PIECES[n]
        if n < 2:
            piece, to = piece_at(b, i - 1, j - 1), down
        elif n < 5:
            piece, to = piece_at(b, i - 3, j - 3), up
        else:
            piece, to = piece_at(b, 1, 1), down
        return remote(piece, piece, y_send.at[b], s_recv.at[b - D0, (0, 1, 1, 1, 1, 2)[n]], col=to)

    def piece_across(b, n):
        piece = piece_at(b, *PIECES[n])
        return remote(piece, piece, d_send.at[b], d_recv.at[b, 1], row=other)

    def spread(b):
        if D0 <= b <= D2:
            for n in (0, 2, 1, 3, 4):
                piece_copy(b, n).start()
            return
        along_y(b, 0, up).start()
        along_y(b, 1, down).start()

    def forward(b):
        if D0 <= b <= D2:
            piece_copy(b, 0).wait_recv()
            piece_copy(b, 5).start()
            arrived(mat.at[b, 0:4, core, :, 0 : 2 * COLS], s_recv.at[b - D0, 1])
            for n in range(5):
                piece_across(b, n).start()
            return
        along_y(b, 0, up).wait_recv()
        onward(b, 0, down, up).start()
        along_y(b, 1, down).wait_recv()
        onward(b, 1, up, down).start()
        across(b, 1).start()
        across(b, 2).start()

    def finish(b):
        if D0 <= b <= D2:
            piece_copy(b, 5).wait_recv()
            piece_across(b, 5).start()
            return
        onward(b, 0, down, up).wait_recv()
        onward(b, 1, up, down).wait_recv()
        across(b, 3).start()

    def strip_shared(b):
        across(b, 0).wait_recv()

    def shared(b):
        if b not in (L3A, L3B, L3C):
            strip_shared(b)
        if D0 <= b <= D2:
            arrived(mat.at[b, 0:6, core, :, 0 : 2 * COLS], d_recv.at[b, 1])
        else:
            arrived(mat.at[b, :, core, :, 0 : 3 * COLS], d_recv.at[b, 1])

    def settle(b):
        if D0 <= b <= D2:
            arrived(mat.at[b, 0:6, core, :, 0 : 2 * COLS], y_send.at[b])
            arrived(mat.at[b, 0:5, core], d_send.at[b])
        else:
            arrived(mat.at[b, 0:6, core], y_send.at[b])
            arrived(mat.at[b, :, core], d_send.at[b])

    mine = 2 * y + core
    half = 2 * y + mod(z, 2)

    def tall(b, t):
        return mat[b, pl.ds(2 * t, 2)].reshape(256, W)

    def wide(b, t):
        return mat[b, :, :, :, cols(t)].reshape(W, 256)

    def strip(b, at):
        return mat[b, :, :, :, cols(at, 128)].reshape(W, 128)

    def strip_at(b, t, at):
        return mat[b, pl.ds(2 * t, 2), :, :, cols(at, 128)].reshape(256, 128)

    def rows_at(t):
        return pl.ds(pl.multiple_of(t * 256, 256), 256)

    def first(t, carry):
        low = strip(L3C, mine)
        at = rows_at(t)
        yab[at, 0:128] = strip_at(L3A, t, mine).astype(F32) - dot(tall(L2A, t), low)
        yab[at, 128:256] = strip_at(L2A, t, half).astype(F32)
        ybb[at, 0:128] = (strip_at(L3B, t, mine).astype(F32) - dot(tall(L2B, t), low)).astype(BF16)
        ybb[at, 128:256] = strip_at(L2B, t, half)
        return carry

    def second(t, carry):
        at = rows_at(t)
        top = yab[at, :] - dot(tall(L1, t), ybb[...])
        yat[0:256, at] = top.T.astype(BF16)
        yat[256:384, at] = strip_at(L1, t, half).astype(F32).T.astype(BF16)
        ybt[:, at] = ybb[at, :].astype(F32).T.astype(BF16)
        yct[:, at] = strip_at(L3C, t, mine).astype(F32).T.astype(BF16)
        return carry

    def put(n, t, value):
        parts = value.T.astype(BF16).reshape(2, 2, XN, PART, 128)
        for q in range(XN):
            for side in range(2):
                res[n, q, side, div(t, 2), mod(t, 2)] = parts[:, side, q]

    def symmetric(left, b, j):
        value = None
        for i in range(YN):
            at = rows_at(mod((y + i), YN))
            if j == 0 or (i, j) in PIECES:
                piece = mat[b, pl.ds(2 * (mod((y + i), YN)), 2), :, :, cols(mod((y + j), YN))].reshape(COLS, COLS)
                term = dot(left[:, at], piece)
            else:
                piece = mat[b, pl.ds(2 * (mod((y + j), YN)), 2), :, :, cols(mod((y + i), YN))].reshape(COLS, COLS)
                term = lax.dot_general(left[:, at], piece, (((1,), (1,)), ((), ())), preferred_element_type=F32)
            value = term if value is None else value + term
        return value

    def root_rows():
        for j in range(YN):
            t = mod((y + j), YN)
            value = symmetric(yat, D0, j)
            za[:, rows_at(t)] = value.astype(BF16)
            put(X3A, t, -value[0:128])
            put(X2A, t, -value[128:256])
            put(X1, t, -value[256:384])

    def one_rows():
        for j in range(YN):
            t = mod((y + j), YN)
            back = dot(za[...], wide(L1, t))
            value = symmetric(ybt, D1, j) - back[0:256]
            zb[:, rows_at(t)] = value.astype(BF16)
            put(X3B, t, -value[0:128])
            put(X2B, t, -value[128:256])
            put(P1, t, back[256:384])

    def two_rows():
        for j in range(YN):
            t = mod((y + j), YN)
            back = dot(za[0:256, :], wide(L2A, t)) + dot(zb[...], wide(L2B, t))
            value = symmetric(yct, D2, j) - back[0:128]
            zc[:, rows_at(t)] = value.astype(BF16)
            put(X3C, t, -value)
            put(P2, t, back[128:256])

    def three_rows(t, carry):
        value = dot(za[0:128, :], wide(L3A, t)) + dot(zb[0:128, :], wide(L3B, t)) + dot(zc[...], wide(L3C, t))
        put(P3, t, value)
        return carry

    gots = (got_a, got_b, got_c, got_d)
    fork = mod((div(z, 2)), 2)

    def batch(n):
        two, one = (core,), (core, slice(None), fork)
        return (
            ((X3A, ()), (X2A, two), (X1, one)),
            ((X3B, ()), (X2B, two), (P1, one)),
            ((X3C, ()), (P2, two)),
            ((P3, ()),),
        )[n]

    def term_copies(n):
        copies = []
        for d in range(1, XN):
            to = mod((pole + d), XN)
            for k, (b, place) in enumerate(batch(n)):
                copies.append(
                    remote(
                        res.at[(b, to) + place],
                        terms.at[(d - 1, b) + place],
                        x_send.at[n, d - 1, k],
                        x_recv.at[n, d - 1, k],
                        pole=to,
                    )
                )
        return copies

    def diag_copies():
        copies = []
        for d in range(1, XN):
            to = mod((pole + d), XN)
            pairs = ((diag_mine.at[:, to], diag_theirs.at[d - 1]), (own_weight, weights.at[d - 1]))
            for k, (src, dst) in enumerate(pairs):
                copies.append(remote(src, dst, p_send.at[d - 1, k], p_recv.at[d - 1, k], pole=to))
        return copies

    def weighted(own, others):
        value = weight_ref[0] * own.astype(F32)
        for d in range(XN - 1):
            value = value + weights[d, 0:1, 0:1] * others(d).astype(F32)
        return value

    def start(copies):
        for copy in copies:
            copy.start()

    def received(copies):
        for copy in copies:
            copy.wait_recv()

    def mask_diagonals():
        own_weight[...] = jnp.full((8, 128), weight_ref[0], F32)
        for n in range(15):
            live = below(rows_of(n), 0) * below(cols_of(n), 1)
            diag_mine[n] = (diag_ref[n] * live).reshape(XN, PART, COLS)

    def sum_diagonals():
        received(diag_copies())
        for n in range(15):
            diag_sum[n] = weighted(diag_mine[n, pole], lambda d: diag_theirs[d, n])

    def sum_terms(n):
        received(term_copies(n))
        for b, place in batch(n):
            at = (b,) + place
            sums[at] = weighted(res[(b, pole) + place], lambda d: terms[(d,) + at])

    def batch_copies(n):
        got = gots[n]
        levels = batch(n)
        copies = []
        for d in range(1, 16):
            to = mod((row + d), 16)
            to_z, side = div(to, 2), mod(to, 2)
            src = sums.at[levels[0][0], side, div(to_z, 4), mod((div(to_z, 2)), 2), mod(to_z, 2)]
            copies.append((src, got.at[z, :, cols(core, 128)], to))
        if len(levels) > 1:
            for d in range(1, ZN):
                to_z = mod((z + d), ZN)
                src = sums.at[levels[1][0], core, div(to_z, 4), mod((div(to_z, 2)), 2), mod(to_z, 2)]
                copies.append((src, got.at[ZN + div(z, 2), :, cols(mod(z, 2), 128)], 2 * to_z + core))
        if len(levels) > 2:
            for dh, dp in ((0, 1), (1, 0), (1, 1)):
                h, p = mod((div(z, 4) + dh), 2), mod((z + dp), 2)
                to_z = 4 * h + 2 * fork + p
                src = sums.at[levels[2][0], core, h, fork, p]
                copies.append((src, got.at[ZN + 4 + div(z, 4), :, cols(mod(z, 2), 128)], 2 * to_z + core))
        return [
            remote(src, dst, o_send.at[n], o_recv.at[n], row=to) for src, dst, to in copies
        ]

    def batch_kept(n):
        places = ((z, core), (ZN + div(z, 2), mod(z, 2)), (ZN + 4 + div(z, 4), mod(z, 2)))
        return [
            pltpu.make_async_copy(
                sums.at[b, core, div(z, 4), fork, mod(z, 2)], gots[n].at[at, :, cols(side, 128)], o_recv.at[n]
            )
            for (b, _), (at, side) in zip(batch(n), places)
        ]

    def leave(n):
        start(batch_copies(n) + batch_kept(n))

    def landed(n):
        arrived(gots[n], o_recv.at[n])

    def order(n):
        got = gots[n]
        if n == 0:
            mine_top[0] = diag_sum[0]
        for i in range(2):
            if n == 0:
                mine_top[1 + 2 * i] = got[12 + i]
            elif n == 1:
                mine_top[2 + 2 * i] = diag_sum[1 + i] + got[12 + i]
        for i in range(4):
            if n < 3:
                value = got[8 + place_two[i]]
                mine_two[i, n] = value + diag_sum[3 + i] if n == 2 else value
        for k in range(8):
            value = got[place_three[k]]
            mine_three[div(k, 2), mod(k, 2), n] = value + diag_sum[7 + k] if n == 3 else value

    part = pl.ds(pl.multiple_of(pole * PART, PART), PART)

    def owner_copies(n):
        copies = []
        for d in range(1, XN):
            to = mod((pole + d), XN)
            pairs = [(mine_three.at[to, :, n], out_three_ref.at[:, n, part])]
            if n < 3:
                pairs.append((mine_two.at[to, n], out_two_ref.at[0, n, part]))
            if n == 1:
                pairs.append((mine_top, top_ref.at[:, part]))
            for k, (src, dst) in enumerate(pairs):
                copies.append(remote(src, dst, g_send.at[n, d - 1, k], g_recv.at[n, d - 1, k], pole=to))
        return copies

    def to_owner(n):
        landed(n)
        order(n)
        start(owner_copies(n))
        for k in range(2):
            out_three_ref[k, n, part] = mine_three[pole, k, n]
        if n < 3:
            out_two_ref[0, n, part] = mine_two[pole, n]
        if n == 1:
            for b in range(5):
                top_ref[b, part] = mine_top[b]

    def stage(body):
        lax.fori_loop(0, 4, body, 0)

    mask(L2A)
    pl.semaphore_wait(barrier, 15 + 2 + 3)
    z_start(L2A)
    mask(L2B)
    mask(L1)
    z_sent(L2A)
    z_start(L2B)
    z_start(L1)
    mask(D0)
    mask(L3C)
    gathered(L2A)
    spread(L2A)
    mask(L3B)
    mask(L3A)
    z_sent(L2B)
    z_start(D0)
    gathered(L2B)
    spread(L2B)
    mask(D1)
    mask(D2)
    z_sent(L1)
    z_start(L3C)
    forward(L2A)
    gathered(L1)
    spread(L1)
    mask_diagonals()
    start(diag_copies())
    z_sent(D0)
    z_start(L3B)
    forward(L2B)
    finish(L2A)
    gathered(D0)
    spread(D0)
    z_sent(L3C)
    z_start(L3A)
    forward(L1)
    finish(L2B)
    gathered(L3C)
    spread(L3C)
    z_sent(L3B)
    z_start(D1)
    forward(D0)
    finish(L1)
    gathered(L3B)
    spread(L3B)
    sum_diagonals()
    z_sent(L3A)
    z_start(D2)
    gathered(L3A)
    shared(L2A)
    shared(L2B)
    for b in (L3A, L3B, L3C):
        strip_shared(b)
    stage(first)
    forward(L3C)
    finish(D0)
    z_sent(D1)
    gathered(D1)
    spread(D1)
    shared(L1)
    stage(second)
    z_sent(D2)
    gathered(D2)
    spread(D2)
    spread(L3A)
    shared(D0)
    root_rows()
    start(term_copies(0))
    forward(L3B)
    finish(L3C)
    forward(D1)
    finish(D1)
    shared(D1)
    one_rows()
    start(term_copies(1))
    forward(D2)
    finish(L3B)
    finish(D2)
    sum_terms(0)
    leave(0)
    shared(D2)
    two_rows()
    start(term_copies(2))
    forward(L3A)
    sum_terms(1)
    leave(1)
    finish(L3A)
    for b in (L3A, L3B, L3C):
        shared(b)
    stage(three_rows)
    start(term_copies(3))
    to_owner(0)
    sum_terms(2)
    leave(2)
    sum_terms(3)
    leave(3)
    to_owner(1)
    to_owner(2)
    to_owner(3)
    for n in range(BATCHES):
        received(owner_copies(n))

    for b in range(9):
        settle(b)
    for n in range(BATCHES):
        if n == 2:
            arrived(got_b.at[0:11], o_send.at[n])
        else:
            arrived(mat.at[0 : (5, 5, 0, 3)[n], 0:5, 0, 0:32, 0:128], o_send.at[n])
        for copy in term_copies(n) + owner_copies(n):
            copy.wait_send()
    for copy in diag_copies():
        copy.wait_send()


VMEM = pl.BlockSpec(memory_space=pltpu.VMEM)
SMEM = pl.BlockSpec(memory_space=pltpu.SMEM)
HBM = pl.BlockSpec(memory_space=pltpu.HBM)
GRANT = 58 * 1024 * 1024


def local(
    lower_one,
    lower_two,
    lower_three,
    diag_inverse,
    pole_weight,
    super_sizes,
    parents,
    keep_two,
    keep_three,
):
    one = lower_one.reshape(2, ROWS, COLS)
    two = lower_two.reshape(4, 2, ROWS, COLS)
    three = lower_three.reshape(8, 3, ROWS, COLS)
    diag = diag_inverse.reshape(15, ROWS, COLS)

    dma = pltpu.SemaphoreType.DMA
    return pl.pallas_call(
        tree,
        out_shape=(
            jax.ShapeDtypeStruct((5, ROWS, COLS), F32),
            jax.ShapeDtypeStruct((1, 3, ROWS, COLS), F32),
            jax.ShapeDtypeStruct((2, 4, ROWS, COLS), F32),
        ),
        in_specs=[HBM] * 4 + [SMEM] * 5,
        out_specs=(VMEM, VMEM, VMEM),
        scratch_shapes=[
            pltpu.VMEM((2, ROWS, COLS), BF16),
            pltpu.VMEM((4, 2, ROWS, COLS), BF16),
            pltpu.VMEM((8, 3, ROWS, COLS), BF16),
            pltpu.VMEM((15, ROWS, COLS), BF16),
            pltpu.VMEM((ZN, 9, ROWS, COLS), BF16),
            pltpu.VMEM((9, ZN, 2, ROWS, W), BF16),
            pltpu.VMEM((9, XN, 2, 2, 2, 2, PART, 128), BF16),
            pltpu.VMEM((W, 256), F32),
            pltpu.VMEM((W, 256), BF16),
            pltpu.VMEM((384, W), BF16),
            pltpu.VMEM((256, W), BF16),
            pltpu.VMEM((128, W), BF16),
            pltpu.VMEM((384, W), BF16),
            pltpu.VMEM((256, W), BF16),
            pltpu.VMEM((128, W), BF16),
            pltpu.VMEM((14, PART, COLS), F32),
            pltpu.VMEM((14, PART, COLS), F32),
            pltpu.VMEM((12, PART, COLS), F32),
            pltpu.VMEM((8, PART, COLS), F32),
            pltpu.VMEM((XN - 1, 9, 2, 2, 2, 2, PART, 128), BF16),
            pltpu.VMEM((9, 2, 2, 2, 2, PART, 128), F32),
            pltpu.VMEM((15, XN, PART, COLS), BF16),
            pltpu.VMEM((XN - 1, 15, PART, COLS), BF16),
            pltpu.VMEM((15, PART, COLS), F32),
            pltpu.VMEM((XN, 3, PART, COLS), F32),
            pltpu.VMEM((XN, 2, 4, PART, COLS), F32),
            pltpu.VMEM((5, PART, COLS), F32),
            pltpu.VMEM((XN - 1, 8, 128), F32),
            pltpu.VMEM((8, 128), F32),
            dma((4,)),
            dma((9,)),
            dma((9,)),
            dma((9,)),
            dma((9, 2)),
            dma((9, 2)),
            dma((9,)),
            dma((9, 2)),
            dma((3, 3)),
            dma((BATCHES,)),
            dma((BATCHES,)),
            dma((BATCHES, XN - 1, 3)),
            dma((BATCHES, XN - 1, 3)),
            dma((XN - 1, 2)),
            dma((XN - 1, 2)),
            dma((BATCHES, XN - 1, 3)),
            dma((BATCHES, XN - 1, 3)),
        ],
        compiler_params=pltpu.CompilerParams(
            collective_id=0, has_side_effects=True, vmem_limit_bytes=GRANT
        ),
    )(one, two, three, diag, super_sizes.T, parents, keep_two, keep_three.T, pole_weight)


def solution(mesh):
    placed = (
        P("pole", None, None, "row", "col"),
        P("pole", None, None, "row", "col"),
        P("pole", None, None, "row", "col"),
        P("pole", None, "row", "col"),
        P("pole"),
        P(),
        P(),
        P(),
        P(),
    )
    return jax.shard_map(
        local,
        mesh=mesh,
        in_specs=placed,
        out_specs=(
            P(None, "row", "col"),
            P("pole", None, "row", "col"),
            P("pole", None, "row", "col"),
        ),
        check_vma=False,
    )
```

```python
import jax
import jax.numpy as jnp
from jax import lax
from jax.experimental import pallas as pl
from jax.experimental.pallas import tpu as pltpu
from jax.sharding import PartitionSpec as P

MESH = pl.DeviceIdType.MESH
F32 = jnp.float32
BF16 = jnp.bfloat16
SUPB = 512
W = 1024
ROWS = 64
COLS = 256
ZN = 8
YN = 4
XN = 4

L2A, L2B, L1, D0, D1, D2, L3A, L3B, L3C = range(9)


def mod(a, n):
    return a % n if isinstance(a, int) else lax.rem(a, n)


def div(a, n):
    return a // n if isinstance(a, int) else lax.div(a, n)


def positions(parents_ref):
    two = [parents_ref[i] for i in range(4)]
    three = [parents_ref[4 + k] for k in range(8)]
    place_two = []
    for i in range(4):
        before = sum([(two[h] == two[i]).astype(jnp.int32) for h in range(i)], jnp.int32(0))
        place_two.append(2 * two[i] + before)
    place_three = []
    for k in range(8):
        before = sum([(three[h] == three[k]).astype(jnp.int32) for h in range(k)], jnp.int32(0))
        above = sum([jnp.where(three[k] == i, place_two[i], 0) for i in range(4)], jnp.int32(0))
        place_three.append(2 * above + before)
    return place_two, place_three


def node_at(places, place):
    return sum([jnp.where(p == place, i, 0) for i, p in enumerate(places)], jnp.int32(0))


def limits(sizes_ref):
    row = lax.axis_index("row") * ROWS
    col = lax.axis_index("col") * COLS
    row_sup, row_at = div(row, SUPB), mod(row, SUPB)
    col_sup, col_at = div(col, SUPB), mod(col, SUPB)
    return (lambda n: sizes_ref[row_sup, n] - row_at), (lambda n: sizes_ref[col_sup, n] - col_at)


def below(limit, axis):
    places = lax.broadcasted_iota(jnp.int32, (ROWS, COLS), axis)
    return jnp.where(places < limit, 1.0, 0.0).astype(BF16)


def dot(a, b):
    return jnp.dot(a, b, preferred_element_type=F32)


X3A, X2A, X1, X3B, X2B, P1, X3C, P2, P3 = range(9)
BATCHES = 4
SHARE = {L2A: 2, L2B: 2, L1: 4, D0: 8, D1: 4, D2: 2, L3A: 1, L3B: 1, L3C: 1}
PART = ROWS // XN


def tree(
    one_hbm,
    two_hbm,
    three_hbm,
    diag_hbm,
    sizes_ref,
    parents_ref,
    keep_two_ref,
    keep_three_ref,
    weight_ref,
    top_ref,
    out_two_ref,
    out_three_ref,
    one_ref,
    two_ref,
    three_ref,
    diag_ref,
    in_ref,
    mat,
    res,
    yab,
    ybb,
    za,
    zb,
    zc,
    acc,
    yat,
    ybt,
    yct,
    got_a,
    got_b,
    got_c,
    got_d,
    terms,
    sums,
    diag_mine,
    diag_theirs,
    diag_sum,
    mine_two,
    mine_three,
    mine_top,
    full_two,
    full_three,
    full_top,
    weights,
    own_weight,
    load_sem,
    z_send,
    z_recv,
    y_send,
    y_recv,
    f_recv,
    d_send,
    d_recv,
    s_recv,
    o_send,
    o_recv,
    x_send,
    x_recv,
    p_send,
    p_recv,
    g_send,
    g_recv,
):
    pole, row, y = lax.axis_index("pole"), lax.axis_index("row"), lax.axis_index("col")
    z, core = div(row, 2), mod(row, 2)
    other = row + 1 - 2 * core
    up, down = mod((y + 1), YN), mod((y + YN - 1), YN)
    far = mod((y + 2), YN)

    loads = [
        pltpu.make_async_copy(src, dst, load_sem.at[n])
        for n, (src, dst) in enumerate(
            ((two_hbm, two_ref), (one_hbm, one_ref), (diag_hbm, diag_ref), (three_hbm, three_ref))
        )
    ]
    for load in loads:
        load.start()

    barrier = pltpu.get_barrier_semaphore()
    for d in range(1, 16):
        pl.semaphore_signal(barrier, inc=1, device_id={"row": mod((row + d), 16)}, device_id_type=MESH)
    for peer in (up, down):
        pl.semaphore_signal(barrier, inc=1, device_id={"col": peer}, device_id_type=MESH)
    for d in range(1, XN):
        pl.semaphore_signal(barrier, inc=1, device_id={"pole": mod((pole + d), XN)}, device_id_type=MESH)

    place_two, place_three = positions(parents_ref)
    rows_of, cols_of = limits(sizes_ref)
    order_two = [node_at(place_two, j) for j in range(4)]
    order_three = [node_at(place_three, k) for k in range(8)]
    r0, c0 = rows_of(0), cols_of(0)
    r1, c1 = [rows_of(1 + i) for i in range(2)], [cols_of(1 + i) for i in range(2)]
    r2, c2 = [rows_of(3 + n) for n in order_two], [cols_of(3 + n) for n in order_two]
    c3 = [cols_of(7 + n) for n in order_three]
    load_of = {L2A: 0, L2B: 0, L1: 1, D0: 2, D1: 2, D2: 2, L3A: 3, L3B: 3, L3C: 3}

    def block(b, to):
        i, j = div(to, 4), div(to, 2)
        n2, n3 = order_two[j], order_three[to]
        if b == L2A:
            return two_ref[n2, 0] * rows[0] * below(c2[j] * keep_two_ref[n2], 1)
        if b == L2B:
            return two_ref[n2, 1] * rows[1 + i] * below(c2[j], 1)
        if b == L1:
            return one_ref[i] * rows[0] * below(c1[i], 1)
        if b == D0:
            return diag_ref[0] * rows[0] * below(c0, 1)
        if b == D1:
            return diag_ref[1 + i] * rows[1 + i] * below(c1[i], 1)
        if b == D2:
            return diag_ref[3 + n2] * rows[3 + j] * below(c2[j], 1)
        if b == L3A:
            return three_ref[n3, 0] * rows[0] * below(c3[to] * keep_three_ref[0, n3], 1)
        if b == L3B:
            return three_ref[n3, 1] * rows[1 + i] * below(c3[to] * keep_three_ref[1, n3], 1)
        return three_ref[n3, 2] * rows[3 + j] * below(c3[to], 1)

    rows, loaded = {}, set()

    def mask(b):
        if load_of[b] not in loaded:
            loaded.add(load_of[b])
            loads[load_of[b]].wait()
        for n in {L2B: (1, 2), D1: (1, 2), D2: (3, 4, 5, 6), L3B: (1, 2), L3C: (3, 4, 5, 6)}.get(b, (0,)):
            if n not in rows:
                rows[n] = below(r0 if n == 0 else r1[n - 1] if n < 3 else r2[n - 3], 0)
        for to in range(0, ZN, SHARE[b]):
            in_ref[to, b] = block(b, to)

    def cols(at, width=COLS):
        return pl.ds(pl.multiple_of(at * width, width), width)

    def remote(src, dst, send, recv, **device):
        return pltpu.make_async_remote_copy(
            src_ref=src, dst_ref=dst, send_sem=send, recv_sem=recv, device_id=device, device_id_type=MESH
        )

    def along_z(b, d):
        to = mod((z + d), ZN)
        return remote(
            in_ref.at[div(to, SHARE[b]) * SHARE[b], b],
            mat.at[b, z, core, :, cols(y)],
            z_send.at[b],
            z_recv.at[b],
            row=2 * to + core,
        )

    def own_copy(b):
        return pltpu.make_async_copy(
            in_ref.at[div(z, SHARE[b]) * SHARE[b], b], mat.at[b, z, core, :, cols(y)], z_recv.at[b]
        )

    def along_y(b, way, to):
        piece = mat.at[b, :, core, :, cols(y)]
        return remote(piece, piece, y_send.at[b], y_recv.at[b, way], col=to)

    def onward(b, way, source, to):
        piece = mat.at[b, pl.ds(4 * way, 4), core, :, cols(source)]
        return remote(piece, piece, y_send.at[b], f_recv.at[b, way], col=to)

    def across(b, n):
        piece = mat.at[b, :, core, :, cols((y, down, up, far)[n])]
        return remote(piece, piece, d_send.at[b], d_recv.at[b, (0, 1, 1, 2)[n]], row=other)

    def z_start(b):
        own_copy(b).start()
        for d in (4, 3, 5, 2, 6, 1, 7):
            along_z(b, d).start()

    def arrived(ref, sem):
        pltpu.make_async_copy(ref, ref, sem).wait()

    def z_sent(b):
        arrived(mat.at[b, 0 : ZN - 1, core, :, cols(y)], z_send.at[b])

    def gathered(b):
        arrived(mat.at[b, :, core, :, cols(y)], z_recv.at[b])
        across(b, 0).start()

    PIECES = ((1, 1), (2, 1), (3, 3), (2, 3), (1, 3), (2, 2))

    def piece_at(b, i, j):
        return mat.at[b, pl.ds(2 * (mod((y + YN + i), YN)), 2), core, :, cols(mod((y + YN + j), YN))]

    def piece_copy(b, n):
        i, j = PIECES[n]
        if n < 2:
            piece, to = piece_at(b, i - 1, j - 1), down
        elif n < 5:
            piece, to = piece_at(b, i - 3, j - 3), up
        else:
            piece, to = piece_at(b, 1, 1), down
        return remote(piece, piece, y_send.at[b], s_recv.at[b - D0, (0, 1, 1, 1, 1, 2)[n]], col=to)

    def piece_across(b, n):
        piece = piece_at(b, *PIECES[n])
        return remote(piece, piece, d_send.at[b], d_recv.at[b, 1], row=other)

    def spread(b):
        if D0 <= b <= D2:
            for n in (0, 2, 1, 3, 4):
                piece_copy(b, n).start()
            return
        along_y(b, 0, up).start()
        along_y(b, 1, down).start()

    def forward(b):
        if D0 <= b <= D2:
            piece_copy(b, 0).wait_recv()
            piece_copy(b, 5).start()
            arrived(mat.at[b, 0:4, core, :, 0 : 2 * COLS], s_recv.at[b - D0, 1])
            for n in range(5):
                piece_across(b, n).start()
            return
        along_y(b, 0, up).wait_recv()
        onward(b, 0, down, up).start()
        along_y(b, 1, down).wait_recv()
        onward(b, 1, up, down).start()
        across(b, 1).start()
        across(b, 2).start()

    def finish(b):
        if D0 <= b <= D2:
            piece_copy(b, 5).wait_recv()
            piece_across(b, 5).start()
            return
        onward(b, 0, down, up).wait_recv()
        onward(b, 1, up, down).wait_recv()
        across(b, 3).start()

    def strip_shared(b):
        across(b, 0).wait_recv()

    def neighbours_shared(b):
        arrived(mat.at[b, :, core, :, 0 : 2 * COLS], d_recv.at[b, 1])

    def shared(b):
        if b not in (L3A, L3B, L3C):
            strip_shared(b)
        if D0 <= b <= D2:
            arrived(mat.at[b, 0:6, core, :, 0 : 2 * COLS], d_recv.at[b, 1])
        else:
            neighbours_shared(b)
            across(b, 3).wait_recv()

    def settle(b):
        if D0 <= b <= D2:
            arrived(mat.at[b, 0:6, core, :, 0 : 2 * COLS], y_send.at[b])
            arrived(mat.at[b, 0:5, core], d_send.at[b])
        else:
            arrived(mat.at[b, 0:6, core], y_send.at[b])
            arrived(mat.at[b, :, core], d_send.at[b])

    mine = 2 * y + core
    half = 2 * y + mod(z, 2)

    def tall(b, t):
        return mat[b, pl.ds(2 * t, 2)].reshape(256, W)

    def wide(b, t):
        return mat[b, :, :, :, cols(t)].reshape(W, 256)

    def strip(b, at):
        return mat[b, :, :, :, cols(at, 128)].reshape(W, 128)

    def strip_at(b, t, at):
        return mat[b, pl.ds(2 * t, 2), :, :, cols(at, 128)].reshape(256, 128)

    def rows_at(t):
        return pl.ds(pl.multiple_of(t * 256, 256), 256)

    def first(t, carry):
        low = strip(L3C, mine)
        at = rows_at(t)
        yab[at, 0:128] = strip_at(L3A, t, mine).astype(F32) - dot(tall(L2A, t), low)
        yab[at, 128:256] = strip_at(L2A, t, half).astype(F32)
        ybb[at, 0:128] = (strip_at(L3B, t, mine).astype(F32) - dot(tall(L2B, t), low)).astype(BF16)
        ybb[at, 128:256] = strip_at(L2B, t, half)
        return carry

    def second(t, carry):
        at = rows_at(t)
        top = yab[at, :] - dot(tall(L1, t), ybb[...])
        yat[0:256, at] = top.T.astype(BF16)
        yat[256:384, at] = strip_at(L1, t, half).astype(F32).T.astype(BF16)
        ybt[:, at] = ybb[at, :].astype(F32).T.astype(BF16)
        yct[:, at] = strip_at(L3C, t, mine).astype(F32).T.astype(BF16)
        return carry

    def put(n, t, value):
        parts = value.T.astype(BF16).reshape(2, 2, XN, PART, 128)
        for q in range(XN):
            for side in range(2):
                res[n, q, side, div(t, 2), mod(t, 2)] = parts[:, side, q]

    def symmetric(left, b, j):
        value = None
        for i in range(YN):
            at = rows_at(mod((y + i), YN))
            if j == 0 or (i, j) in PIECES:
                piece = mat[b, pl.ds(2 * (mod((y + i), YN)), 2), :, :, cols(mod((y + j), YN))].reshape(COLS, COLS)
                term = dot(left[:, at], piece)
            else:
                piece = mat[b, pl.ds(2 * (mod((y + j), YN)), 2), :, :, cols(mod((y + i), YN))].reshape(COLS, COLS)
                term = lax.dot_general(left[:, at], piece, (((1,), (1,)), ((), ())), preferred_element_type=F32)
            value = term if value is None else value + term
        return value

    def root_rows():
        for j in range(YN):
            t = mod((y + j), YN)
            value = symmetric(yat, D0, j)
            za[:, rows_at(t)] = value.astype(BF16)
            put(X3A, t, -value[0:128])
            put(X2A, t, -value[128:256])
            put(X1, t, -value[256:384])

    def one_rows():
        for j in range(YN):
            t = mod((y + j), YN)
            back = dot(za[...], wide(L1, t))
            value = symmetric(ybt, D1, j) - back[0:256]
            zb[:, rows_at(t)] = value.astype(BF16)
            put(X3B, t, -value[0:128])
            put(X2B, t, -value[128:256])
            put(P1, t, back[256:384])

    def two_rows():
        for j in range(YN):
            t = mod((y + j), YN)
            back = dot(za[0:256, :], wide(L2A, t)) + dot(zb[...], wide(L2B, t))
            value = symmetric(yct, D2, j) - back[0:128]
            zc[:, rows_at(t)] = value.astype(BF16)
            put(X3C, t, -value)
            put(P2, t, back[128:256])

    def three_begin(t, carry):
        acc[:, rows_at(t)] = dot(zb[0:128, :], wide(L3B, t)) + dot(zc[...], wide(L3C, t))
        return carry

    def three_rows(j):
        t = mod(y + j, YN)
        put(P3, t, acc[:, rows_at(t)] + dot(za[0:128, :], wide(L3A, t)))

    gots = (got_a, got_b, got_c, got_d)
    fork = mod((div(z, 2)), 2)

    def batch(n):
        two, one = (core,), (core, slice(None), fork)
        return (
            ((X3A, ()), (X2A, two), (X1, one)),
            ((X3B, ()), (X2B, two), (P1, one)),
            ((X3C, ()), (P2, two)),
        )[n]

    def term_copies(n):
        copies = []
        for d in range(1, XN):
            to = mod((pole + d), XN)
            for k, (b, place) in enumerate(batch(n)):
                copies.append(
                    remote(
                        res.at[(b, to) + place],
                        terms.at[(d - 1, b) + place],
                        x_send.at[n, d - 1, k],
                        x_recv.at[n, d - 1, k],
                        pole=to,
                    )
                )
        return copies

    def diag_copies():
        copies = []
        for d in range(1, XN):
            to = mod((pole + d), XN)
            pairs = ((diag_mine.at[:, to], diag_theirs.at[d - 1]), (own_weight, weights.at[d - 1]))
            for k, (src, dst) in enumerate(pairs):
                copies.append(remote(src, dst, p_send.at[d - 1, k], p_recv.at[d - 1, k], pole=to))
        return copies

    def weighted(own, others):
        value = weight_ref[0] * own.astype(F32)
        for d in range(XN - 1):
            value = value + weights[d, 0:1, 0:1] * others(d).astype(F32)
        return value

    def start(copies):
        for copy in copies:
            copy.start()

    def received(copies):
        for copy in copies:
            copy.wait_recv()

    def mask_diagonals():
        own_weight[...] = jnp.full((8, 128), weight_ref[0], F32)
        for n in range(15):
            live = below(rows_of(n), 0) * below(cols_of(n), 1)
            diag_mine[n] = (diag_ref[n] * live).reshape(XN, PART, COLS)

    def sum_diagonals():
        received(diag_copies())
        for n in range(15):
            diag_sum[n] = weighted(diag_mine[n, pole], lambda d: diag_theirs[d, n])

    def sum_terms(n):
        received(term_copies(n))
        for b, place in batch(n):
            at = (b,) + place
            sums[at] = weighted(res[(b, pole) + place], lambda d: terms[(d,) + at]).astype(BF16)

    def quarter_place(j):
        t = mod(y + j, YN)
        return (slice(None), div(t, 2), mod(t, 2))

    def quarter_copies(j):
        place = quarter_place(j)
        copies = []
        for d in range(1, XN):
            src, dst = (P3, mod(pole + d, XN)) + place, (d - 1, P3) + place
            copies.append(
                remote(
                    res.at[src], terms.at[dst], x_send.at[3, d - 1, j], x_recv.at[3, d - 1, j], pole=mod(pole + d, XN)
                )
            )
        return copies

    def leave_quarter(j):
        received(quarter_copies(j))
        place = quarter_place(j)
        sums[(P3,) + place] = weighted(res[(P3, pole) + place], lambda d: terms[(d, P3) + place]).astype(BF16)
        for p in range(2):
            for side in range(2):
                to = 4 * mod(y + j, YN) + 2 * p + side
                src = sums.at[P3, side, place[1], place[2], p]
                dst = got_d.at[z, :, cols(core, 128)]

                @pl.when(to != row)
                def _():
                    remote(src, dst, o_send.at[3], o_recv.at[3], row=to).start()

                @pl.when(to == row)
                def _():
                    pltpu.make_async_copy(src, dst, o_recv.at[3]).start()

    def batch_copies(n):
        got = gots[n]
        levels = batch(n)
        copies = []
        for d in range(1, 16):
            to = mod((row + d), 16)
            to_z, side = div(to, 2), mod(to, 2)
            src = sums.at[levels[0][0], side, div(to_z, 4), mod((div(to_z, 2)), 2), mod(to_z, 2)]
            copies.append((src, got.at[z, :, cols(core, 128)], to))
        if len(levels) > 1:
            for d in range(1, ZN):
                to_z = mod((z + d), ZN)
                src = sums.at[levels[1][0], core, div(to_z, 4), mod((div(to_z, 2)), 2), mod(to_z, 2)]
                copies.append((src, got.at[ZN + div(z, 2), :, cols(mod(z, 2), 128)], 2 * to_z + core))
        if len(levels) > 2:
            for dh, dp in ((0, 1), (1, 0), (1, 1)):
                h, p = mod((div(z, 4) + dh), 2), mod((z + dp), 2)
                to_z = 4 * h + 2 * fork + p
                src = sums.at[levels[2][0], core, h, fork, p]
                copies.append((src, got.at[ZN + 4 + div(z, 4), :, cols(mod(z, 2), 128)], 2 * to_z + core))
        return [
            remote(src, dst, o_send.at[n], o_recv.at[n], row=to) for src, dst, to in copies
        ]

    def batch_kept(n):
        places = ((z, core), (ZN + div(z, 2), mod(z, 2)), (ZN + 4 + div(z, 4), mod(z, 2)))
        return [
            pltpu.make_async_copy(
                sums.at[b, core, div(z, 4), fork, mod(z, 2)], gots[n].at[at, :, cols(side, 128)], o_recv.at[n]
            )
            for (b, _), (at, side) in zip(batch(n), places)
        ]

    def leave(n):
        start(batch_copies(n) + batch_kept(n))

    def landed(n):
        arrived(gots[n], o_recv.at[n])

    def order(n):
        got = gots[n]

        def with_diagonal(value, node):
            return (value.astype(F32) + diag_sum[node]).astype(BF16)

        if n == 0:
            mine_top[0] = diag_sum[0].astype(BF16)
        for i in range(2):
            if n == 0:
                mine_top[1 + 2 * i] = got[12 + i]
            elif n == 1:
                mine_top[2 + 2 * i] = with_diagonal(got[12 + i], 1 + i)
        for i in range(4):
            if n < 3:
                value = got[8 + place_two[i]]
                mine_two[i, n] = with_diagonal(value, 3 + i) if n == 2 else value
        for k in range(8):
            value = got[place_three[k]]
            mine_three[k // 2, k % 2, n] = with_diagonal(value, 7 + k) if n == 3 else value

    def owner_copies(n):
        copies = []
        for d in range(1, XN):
            to = mod((pole + d), XN)
            pairs = [(mine_three.at[to, :, n], full_three.at[pole, :, n])]
            if n < 3:
                pairs.append((mine_two.at[to, n], full_two.at[pole, n]))
            if n == 1:
                pairs.append((mine_top, full_top.at[pole]))
            for k, (src, dst) in enumerate(pairs):
                copies.append(remote(src, dst, g_send.at[n, d - 1, k], g_recv.at[n, d - 1, k], pole=to))
        return copies

    def to_owner(n):
        landed(n)
        order(n)
        start(owner_copies(n))
        full_three[pole, :, n] = mine_three[pole, :, n]
        if n < 3:
            full_two[pole, n] = mine_two[pole, n]
        if n == 1:
            full_top[pole] = mine_top[...]

    def write(n):
        received(owner_copies(n))
        for q in range(XN):
            part = slice(q * PART, (q + 1) * PART)
            for k in range(2):
                out_three_ref[k, n, part] = full_three[q, k, n].astype(F32)
            if n < 3:
                out_two_ref[0, n, part] = full_two[q, n].astype(F32)
            if n == 1:
                for b in range(5):
                    top_ref[b, part] = full_top[q, b].astype(F32)

    def stage(body):
        lax.fori_loop(0, 4, body, 0)

    mask(L2A)
    pl.semaphore_wait(barrier, 15 + 2 + 3)
    z_start(L2A)
    mask(L2B)
    mask(L1)
    z_sent(L2A)
    z_start(L2B)
    z_start(L1)
    mask(D0)
    mask(L3C)
    gathered(L2A)
    spread(L2A)
    mask(L3B)
    mask(L3A)
    z_sent(L2B)
    z_start(D0)
    gathered(L2B)
    spread(L2B)
    mask(D1)
    mask(D2)
    z_sent(L1)
    z_start(L3C)
    forward(L2A)
    gathered(L1)
    spread(L1)
    mask_diagonals()
    start(diag_copies())
    z_sent(D0)
    z_start(L3B)
    forward(L2B)
    finish(L2A)
    gathered(D0)
    spread(D0)
    z_sent(L3C)
    z_start(L3A)
    forward(L1)
    finish(L2B)
    gathered(L3C)
    spread(L3C)
    z_sent(L3B)
    z_start(D1)
    forward(D0)
    finish(L1)
    gathered(L3B)
    spread(L3B)
    sum_diagonals()
    z_sent(L3A)
    z_start(D2)
    gathered(L3A)
    shared(L2A)
    shared(L2B)
    for b in (L3A, L3B, L3C):
        strip_shared(b)
    stage(first)
    forward(L3C)
    finish(D0)
    z_sent(D1)
    gathered(D1)
    spread(D1)
    shared(L1)
    stage(second)
    z_sent(D2)
    gathered(D2)
    spread(D2)
    spread(L3A)
    shared(D0)
    root_rows()
    start(term_copies(0))
    forward(L3B)
    finish(L3C)
    sum_terms(0)
    leave(0)
    forward(D1)
    finish(D1)
    shared(D1)
    one_rows()
    start(term_copies(1))
    forward(D2)
    finish(L3B)
    finish(D2)
    shared(D2)
    two_rows()
    start(term_copies(2))
    forward(L3A)
    shared(L3B)
    shared(L3C)
    stage(three_begin)
    neighbours_shared(L3A)
    for j in (0, 1, 3):
        three_rows(j)
        start(quarter_copies(j))
    sum_terms(1)
    leave(1)
    finish(L3A)
    to_owner(0)
    across(L3A, 3).wait_recv()
    three_rows(2)
    start(quarter_copies(2))
    for j in (0, 1, 3):
        leave_quarter(j)
    sum_terms(2)
    leave(2)
    leave_quarter(2)
    to_owner(1)
    to_owner(3)
    to_owner(2)
    for n in (0, 1, 3, 2):
        write(n)

    for b in range(9):
        settle(b)
    for n in range(BATCHES):
        if n == 2:
            arrived(got_b.at[0:11], o_send.at[n])
        else:
            arrived(mat.at[0 : (5, 5, 0, 3)[n], 0:5, 0, 0:PART, 0:128], o_send.at[n])
        for copy in (term_copies(n) if n < 3 else []) + owner_copies(n):
            copy.wait_send()
    for j in range(YN):
        for copy in quarter_copies(j):
            copy.wait_send()
    for copy in diag_copies():
        copy.wait_send()


VMEM = pl.BlockSpec(memory_space=pltpu.VMEM)
SMEM = pl.BlockSpec(memory_space=pltpu.SMEM)
HBM = pl.BlockSpec(memory_space=pltpu.HBM)
GRANT = 58 * 1024 * 1024


def local(
    lower_one,
    lower_two,
    lower_three,
    diag_inverse,
    pole_weight,
    super_sizes,
    parents,
    keep_two,
    keep_three,
):
    one = lower_one.reshape(2, ROWS, COLS)
    two = lower_two.reshape(4, 2, ROWS, COLS)
    three = lower_three.reshape(8, 3, ROWS, COLS)
    diag = diag_inverse.reshape(15, ROWS, COLS)

    dma = pltpu.SemaphoreType.DMA
    return pl.pallas_call(
        tree,
        out_shape=(
            jax.ShapeDtypeStruct((5, ROWS, COLS), F32),
            jax.ShapeDtypeStruct((1, 3, ROWS, COLS), F32),
            jax.ShapeDtypeStruct((2, 4, ROWS, COLS), F32),
        ),
        in_specs=[HBM] * 4 + [SMEM] * 5,
        out_specs=(VMEM, VMEM, VMEM),
        scratch_shapes=[
            pltpu.VMEM((2, ROWS, COLS), BF16),
            pltpu.VMEM((4, 2, ROWS, COLS), BF16),
            pltpu.VMEM((8, 3, ROWS, COLS), BF16),
            pltpu.VMEM((15, ROWS, COLS), BF16),
            pltpu.VMEM((ZN, 9, ROWS, COLS), BF16),
            pltpu.VMEM((9, ZN, 2, ROWS, W), BF16),
            pltpu.VMEM((9, XN, 2, 2, 2, 2, PART, 128), BF16),
            pltpu.VMEM((W, 256), F32),
            pltpu.VMEM((W, 256), BF16),
            pltpu.VMEM((384, W), BF16),
            pltpu.VMEM((256, W), BF16),
            pltpu.VMEM((128, W), BF16),
            pltpu.VMEM((128, W), F32),
            pltpu.VMEM((384, W), BF16),
            pltpu.VMEM((256, W), BF16),
            pltpu.VMEM((128, W), BF16),
            pltpu.VMEM((14, PART, COLS), BF16),
            pltpu.VMEM((14, PART, COLS), BF16),
            pltpu.VMEM((12, PART, COLS), BF16),
            pltpu.VMEM((8, PART, COLS), BF16),
            pltpu.VMEM((XN - 1, 9, 2, 2, 2, 2, PART, 128), BF16),
            pltpu.VMEM((9, 2, 2, 2, 2, PART, 128), BF16),
            pltpu.VMEM((15, XN, PART, COLS), BF16),
            pltpu.VMEM((XN - 1, 15, PART, COLS), BF16),
            pltpu.VMEM((15, PART, COLS), F32),
            pltpu.VMEM((XN, 3, PART, COLS), BF16),
            pltpu.VMEM((XN, 2, 4, PART, COLS), BF16),
            pltpu.VMEM((5, PART, COLS), BF16),
            pltpu.VMEM((XN, 3, PART, COLS), BF16),
            pltpu.VMEM((XN, 2, 4, PART, COLS), BF16),
            pltpu.VMEM((XN, 5, PART, COLS), BF16),
            pltpu.VMEM((XN - 1, 8, 128), F32),
            pltpu.VMEM((8, 128), F32),
            dma((4,)),
            dma((9,)),
            dma((9,)),
            dma((9,)),
            dma((9, 2)),
            dma((9, 2)),
            dma((9,)),
            dma((9, 3)),
            dma((3, 3)),
            dma((BATCHES,)),
            dma((BATCHES,)),
            dma((BATCHES, XN - 1, 4)),
            dma((BATCHES, XN - 1, 4)),
            dma((XN - 1, 2)),
            dma((XN - 1, 2)),
            dma((BATCHES, XN - 1, 3)),
            dma((BATCHES, XN - 1, 3)),
        ],
        compiler_params=pltpu.CompilerParams(
            collective_id=0, has_side_effects=True, vmem_limit_bytes=GRANT
        ),
    )(one, two, three, diag, super_sizes.T, parents, keep_two, keep_three.T, pole_weight)


def solution(mesh):
    placed = (
        P("pole", None, None, "row", "col"),
        P("pole", None, None, "row", "col"),
        P("pole", None, None, "row", "col"),
        P("pole", None, "row", "col"),
        P("pole"),
        P(),
        P(),
        P(),
        P(),
    )
    return jax.shard_map(
        local,
        mesh=mesh,
        in_specs=placed,
        out_specs=(
            P(None, "row", "col"),
            P("pole", None, "row", "col"),
            P("pole", None, "row", "col"),
        ),
        check_vma=False,
    )
```

```python
import jax
import jax.numpy as jnp
from jax import lax
from jax.experimental import pallas as pl
from jax.experimental.pallas import tpu as pltpu
from jax.sharding import PartitionSpec as P

MESH = pl.DeviceIdType.MESH
F32 = jnp.float32
BF16 = jnp.bfloat16
SUPB = 512
W = 1024
ROWS = 64
COLS = 256
ZN = 8
YN = 4
XN = 4

L2A, L2B, L1, D0, D1, D2, L3A, L3B, L3C = range(9)


def mod(a, n):
    return a % n if isinstance(a, int) else lax.rem(a, n)


def div(a, n):
    return a // n if isinstance(a, int) else lax.div(a, n)


def positions(parents_ref):
    two = [parents_ref[i] for i in range(4)]
    three = [parents_ref[4 + k] for k in range(8)]
    place_two = []
    for i in range(4):
        before = sum([(two[h] == two[i]).astype(jnp.int32) for h in range(i)], jnp.int32(0))
        place_two.append(2 * two[i] + before)
    place_three = []
    for k in range(8):
        before = sum([(three[h] == three[k]).astype(jnp.int32) for h in range(k)], jnp.int32(0))
        above = sum([jnp.where(three[k] == i, place_two[i], 0) for i in range(4)], jnp.int32(0))
        place_three.append(2 * above + before)
    return place_two, place_three


def node_at(places, place):
    return sum([jnp.where(p == place, i, 0) for i, p in enumerate(places)], jnp.int32(0))


def limits(sizes_ref):
    row = lax.axis_index("row") * ROWS
    col = lax.axis_index("col") * COLS
    row_sup, row_at = div(row, SUPB), mod(row, SUPB)
    col_sup, col_at = div(col, SUPB), mod(col, SUPB)
    return (lambda n: sizes_ref[row_sup, n] - row_at), (lambda n: sizes_ref[col_sup, n] - col_at)


def below(limit, axis):
    places = lax.broadcasted_iota(jnp.int32, (ROWS, COLS), axis)
    return jnp.where(places < limit, 1.0, 0.0).astype(BF16)


def dot(a, b):
    return jnp.dot(a, b, preferred_element_type=F32)


X3A, X2A, X1, X3B, X2B, P1, X3C, P2, P3 = range(9)
BATCHES = 4
SHARE = {L2A: 2, L2B: 2, L1: 4, D0: 8, D1: 4, D2: 2, L3A: 1, L3B: 1, L3C: 1}
PART = ROWS // XN


def tree(
    one_hbm,
    two_hbm,
    three_hbm,
    diag_hbm,
    sizes_ref,
    parents_ref,
    keep_two_ref,
    keep_three_ref,
    weight_ref,
    full_two,
    full_three,
    full_top,
    one_ref,
    two_ref,
    three_ref,
    diag_ref,
    in_ref,
    mat,
    res,
    yab,
    ybb,
    za,
    zb,
    zc,
    acc,
    yat,
    ybt,
    yct,
    got_a,
    got_b,
    got_c,
    got_d,
    terms,
    sums,
    diag_mine,
    diag_theirs,
    diag_sum,
    mine_two,
    mine_three,
    mine_top,
    weights,
    own_weight,
    load_sem,
    z_send,
    z_recv,
    y_send,
    y_recv,
    f_recv,
    d_send,
    d_recv,
    s_recv,
    o_send,
    o_recv,
    x_send,
    x_recv,
    p_send,
    p_recv,
    g_send,
    g_recv,
):
    pole, row, y = lax.axis_index("pole"), lax.axis_index("row"), lax.axis_index("col")
    z, core = div(row, 2), mod(row, 2)
    other = row + 1 - 2 * core
    up, down = mod((y + 1), YN), mod((y + YN - 1), YN)
    far = mod((y + 2), YN)

    loads = [
        pltpu.make_async_copy(src, dst, load_sem.at[n])
        for n, (src, dst) in enumerate(
            ((two_hbm, two_ref), (one_hbm, one_ref), (diag_hbm, diag_ref), (three_hbm, three_ref))
        )
    ]
    for load in loads:
        load.start()

    barrier = pltpu.get_barrier_semaphore()
    for d in range(1, 16):
        pl.semaphore_signal(barrier, inc=1, device_id={"row": mod((row + d), 16)}, device_id_type=MESH)
    for peer in (up, down):
        pl.semaphore_signal(barrier, inc=1, device_id={"col": peer}, device_id_type=MESH)
    for d in range(1, XN):
        pl.semaphore_signal(barrier, inc=1, device_id={"pole": mod((pole + d), XN)}, device_id_type=MESH)

    place_two, place_three = positions(parents_ref)
    rows_of, cols_of = limits(sizes_ref)
    order_two = [node_at(place_two, j) for j in range(4)]
    order_three = [node_at(place_three, k) for k in range(8)]
    r0, c0 = rows_of(0), cols_of(0)
    r1, c1 = [rows_of(1 + i) for i in range(2)], [cols_of(1 + i) for i in range(2)]
    r2, c2 = [rows_of(3 + n) for n in order_two], [cols_of(3 + n) for n in order_two]
    c3 = [cols_of(7 + n) for n in order_three]
    load_of = {L2A: 0, L2B: 0, L1: 1, D0: 2, D1: 2, D2: 2, L3A: 3, L3B: 3, L3C: 3}

    def block(b, to):
        i, j = div(to, 4), div(to, 2)
        n2, n3 = order_two[j], order_three[to]
        if b == L2A:
            return two_ref[n2, 0] * rows[0] * below(c2[j] * keep_two_ref[n2], 1)
        if b == L2B:
            return two_ref[n2, 1] * rows[1 + i] * below(c2[j], 1)
        if b == L1:
            return one_ref[i] * rows[0] * below(c1[i], 1)
        if b == D0:
            return diag_ref[0] * rows[0] * below(c0, 1)
        if b == D1:
            return diag_ref[1 + i] * rows[1 + i] * below(c1[i], 1)
        if b == D2:
            return diag_ref[3 + n2] * rows[3 + j] * below(c2[j], 1)
        if b == L3A:
            return three_ref[n3, 0] * rows[0] * below(c3[to] * keep_three_ref[0, n3], 1)
        if b == L3B:
            return three_ref[n3, 1] * rows[1 + i] * below(c3[to] * keep_three_ref[1, n3], 1)
        return three_ref[n3, 2] * rows[3 + j] * below(c3[to], 1)

    rows, loaded = {}, set()

    def mask(b):
        if load_of[b] not in loaded:
            loaded.add(load_of[b])
            loads[load_of[b]].wait()
        for n in {L2B: (1, 2), D1: (1, 2), D2: (3, 4, 5, 6), L3B: (1, 2), L3C: (3, 4, 5, 6)}.get(b, (0,)):
            if n not in rows:
                rows[n] = below(r0 if n == 0 else r1[n - 1] if n < 3 else r2[n - 3], 0)
        for to in range(0, ZN, SHARE[b]):
            in_ref[to, b] = block(b, to)

    def cols(at, width=COLS):
        return pl.ds(pl.multiple_of(at * width, width), width)

    def remote(src, dst, send, recv, **device):
        return pltpu.make_async_remote_copy(
            src_ref=src, dst_ref=dst, send_sem=send, recv_sem=recv, device_id=device, device_id_type=MESH
        )

    def along_z(b, d):
        to = mod((z + d), ZN)
        return remote(
            in_ref.at[div(to, SHARE[b]) * SHARE[b], b],
            mat.at[b, z, core, :, cols(y)],
            z_send.at[b],
            z_recv.at[b],
            row=2 * to + core,
        )

    def own_copy(b):
        return pltpu.make_async_copy(
            in_ref.at[div(z, SHARE[b]) * SHARE[b], b], mat.at[b, z, core, :, cols(y)], z_recv.at[b]
        )

    def along_y(b, way, to):
        piece = mat.at[b, :, core, :, cols(y)]
        return remote(piece, piece, y_send.at[b], y_recv.at[b, way], col=to)

    def onward(b, way, source, to):
        piece = mat.at[b, pl.ds(4 * way, 4), core, :, cols(source)]
        return remote(piece, piece, y_send.at[b], f_recv.at[b, way], col=to)

    def across(b, n):
        piece = mat.at[b, :, core, :, cols((y, down, up, far)[n])]
        return remote(piece, piece, d_send.at[b], d_recv.at[b, (0, 1, 1, 2)[n]], row=other)

    def z_start(b):
        own_copy(b).start()
        for d in (4, 3, 5, 2, 6, 1, 7):
            along_z(b, d).start()

    def arrived(ref, sem):
        pltpu.make_async_copy(ref, ref, sem).wait()

    def z_sent(b):
        arrived(mat.at[b, 0 : ZN - 1, core, :, cols(y)], z_send.at[b])

    def gathered(b):
        arrived(mat.at[b, :, core, :, cols(y)], z_recv.at[b])
        across(b, 0).start()

    PIECES = ((1, 1), (2, 1), (3, 3), (2, 3), (1, 3), (2, 2))

    def piece_at(b, i, j):
        return mat.at[b, pl.ds(2 * (mod((y + YN + i), YN)), 2), core, :, cols(mod((y + YN + j), YN))]

    def piece_copy(b, n):
        i, j = PIECES[n]
        if n < 2:
            piece, to = piece_at(b, i - 1, j - 1), down
        elif n < 5:
            piece, to = piece_at(b, i - 3, j - 3), up
        else:
            piece, to = piece_at(b, 1, 1), down
        return remote(piece, piece, y_send.at[b], s_recv.at[b - D0, (0, 1, 1, 1, 1, 2)[n]], col=to)

    def piece_across(b, n):
        piece = piece_at(b, *PIECES[n])
        return remote(piece, piece, d_send.at[b], d_recv.at[b, 1], row=other)

    def spread(b):
        if D0 <= b <= D2:
            for n in (0, 2, 1, 3, 4):
                piece_copy(b, n).start()
            return
        along_y(b, 0, up).start()
        along_y(b, 1, down).start()

    def forward(b):
        if D0 <= b <= D2:
            piece_copy(b, 0).wait_recv()
            piece_copy(b, 5).start()
            arrived(mat.at[b, 0:4, core, :, 0 : 2 * COLS], s_recv.at[b - D0, 1])
            for n in range(5):
                piece_across(b, n).start()
            return
        along_y(b, 0, up).wait_recv()
        onward(b, 0, down, up).start()
        along_y(b, 1, down).wait_recv()
        onward(b, 1, up, down).start()
        across(b, 1).start()
        across(b, 2).start()

    def finish(b):
        if D0 <= b <= D2:
            piece_copy(b, 5).wait_recv()
            piece_across(b, 5).start()
            return
        onward(b, 0, down, up).wait_recv()
        onward(b, 1, up, down).wait_recv()
        across(b, 3).start()

    def strip_shared(b):
        across(b, 0).wait_recv()

    def neighbours_shared(b):
        arrived(mat.at[b, :, core, :, 0 : 2 * COLS], d_recv.at[b, 1])

    def shared(b):
        if b not in (L3A, L3B, L3C):
            strip_shared(b)
        if D0 <= b <= D2:
            arrived(mat.at[b, 0:6, core, :, 0 : 2 * COLS], d_recv.at[b, 1])
        else:
            neighbours_shared(b)
            across(b, 3).wait_recv()

    def settle(b):
        if D0 <= b <= D2:
            arrived(mat.at[b, 0:6, core, :, 0 : 2 * COLS], y_send.at[b])
            arrived(mat.at[b, 0:5, core], d_send.at[b])
        else:
            arrived(mat.at[b, 0:6, core], y_send.at[b])
            arrived(mat.at[b, :, core], d_send.at[b])

    mine = 2 * y + core
    half = 2 * y + mod(z, 2)

    def tall(b, t):
        return mat[b, pl.ds(2 * t, 2)].reshape(256, W)

    def wide(b, t):
        return mat[b, :, :, :, cols(t)].reshape(W, 256)

    def strip(b, at):
        return mat[b, :, :, :, cols(at, 128)].reshape(W, 128)

    def strip_at(b, t, at):
        return mat[b, pl.ds(2 * t, 2), :, :, cols(at, 128)].reshape(256, 128)

    def rows_at(t):
        return pl.ds(pl.multiple_of(t * 256, 256), 256)

    def first(t, carry):
        low = strip(L3C, mine)
        at = rows_at(t)
        yab[at, 0:128] = strip_at(L3A, t, mine).astype(F32) - dot(tall(L2A, t), low)
        yab[at, 128:256] = strip_at(L2A, t, half).astype(F32)
        ybb[at, 0:128] = (strip_at(L3B, t, mine).astype(F32) - dot(tall(L2B, t), low)).astype(BF16)
        ybb[at, 128:256] = strip_at(L2B, t, half)
        return carry

    def second(t, carry):
        at = rows_at(t)
        top = yab[at, :] - dot(tall(L1, t), ybb[...])
        yat[0:256, at] = top.T.astype(BF16)
        yat[256:384, at] = strip_at(L1, t, half).astype(F32).T.astype(BF16)
        ybt[:, at] = ybb[at, :].astype(F32).T.astype(BF16)
        yct[:, at] = strip_at(L3C, t, mine).astype(F32).T.astype(BF16)
        return carry

    def put(n, t, value):
        parts = value.T.astype(BF16).reshape(2, 2, XN, PART, 128)
        for q in range(XN):
            for side in range(2):
                res[n, q, side, div(t, 2), mod(t, 2)] = parts[:, side, q]

    def symmetric(left, b, j):
        value = None
        for i in range(YN):
            at = rows_at(mod((y + i), YN))
            if j == 0 or (i, j) in PIECES:
                piece = mat[b, pl.ds(2 * (mod((y + i), YN)), 2), :, :, cols(mod((y + j), YN))].reshape(COLS, COLS)
                term = dot(left[:, at], piece)
            else:
                piece = mat[b, pl.ds(2 * (mod((y + j), YN)), 2), :, :, cols(mod((y + i), YN))].reshape(COLS, COLS)
                term = lax.dot_general(left[:, at], piece, (((1,), (1,)), ((), ())), preferred_element_type=F32)
            value = term if value is None else value + term
        return value

    def root_rows():
        for j in range(YN):
            t = mod((y + j), YN)
            value = symmetric(yat, D0, j)
            za[:, rows_at(t)] = value.astype(BF16)
            put(X3A, t, -value[0:128])
            put(X2A, t, -value[128:256])
            put(X1, t, -value[256:384])

    def one_rows():
        for j in range(YN):
            t = mod((y + j), YN)
            back = dot(za[...], wide(L1, t))
            value = symmetric(ybt, D1, j) - back[0:256]
            zb[:, rows_at(t)] = value.astype(BF16)
            put(X3B, t, -value[0:128])
            put(X2B, t, -value[128:256])
            put(P1, t, back[256:384])

    def two_rows():
        for j in range(YN):
            t = mod((y + j), YN)
            back = dot(za[0:256, :], wide(L2A, t)) + dot(zb[...], wide(L2B, t))
            value = symmetric(yct, D2, j) - back[0:128]
            zc[:, rows_at(t)] = value.astype(BF16)
            put(X3C, t, -value)
            put(P2, t, back[128:256])

    def three_begin(t, carry):
        acc[:, rows_at(t)] = dot(zb[0:128, :], wide(L3B, t)) + dot(zc[...], wide(L3C, t))
        return carry

    def three_rows(j):
        t = mod(y + j, YN)
        put(P3, t, acc[:, rows_at(t)] + dot(za[0:128, :], wide(L3A, t)))

    gots = (got_a, got_b, got_c, got_d)
    fork = mod((div(z, 2)), 2)

    def batch(n):
        two, one = (core,), (core, slice(None), fork)
        return (
            ((X3A, ()), (X2A, two), (X1, one)),
            ((X3B, ()), (X2B, two), (P1, one)),
            ((X3C, ()), (P2, two)),
        )[n]

    def term_copies(n):
        copies = []
        for d in range(1, XN):
            to = mod((pole + d), XN)
            for k, (b, place) in enumerate(batch(n)):
                copies.append(
                    remote(
                        res.at[(b, to) + place],
                        terms.at[(d - 1, b) + place],
                        x_send.at[n, d - 1, k],
                        x_recv.at[n, d - 1, k],
                        pole=to,
                    )
                )
        return copies

    def diag_copies():
        copies = []
        for d in range(1, XN):
            to = mod((pole + d), XN)
            pairs = ((diag_mine.at[:, to], diag_theirs.at[d - 1]), (own_weight, weights.at[d - 1]))
            for k, (src, dst) in enumerate(pairs):
                copies.append(remote(src, dst, p_send.at[d - 1, k], p_recv.at[d - 1, k], pole=to))
        return copies

    def weighted(own, others):
        value = weight_ref[0] * own.astype(F32)
        for d in range(XN - 1):
            value = value + weights[d, 0:1, 0:1] * others(d).astype(F32)
        return value

    def start(copies):
        for copy in copies:
            copy.start()

    def sent(copies):
        for copy in copies:
            copy.wait_send()

    def received(copies):
        for copy in copies:
            copy.wait_recv()

    def mask_diagonals():
        own_weight[...] = jnp.full((8, 128), weight_ref[0], F32)
        for n in range(15):
            live = below(rows_of(n), 0) * below(cols_of(n), 1)
            diag_mine[n] = (diag_ref[n] * live).reshape(XN, PART, COLS)

    def sum_diagonals():
        received(diag_copies())
        for n in range(15):
            diag_sum[n] = weighted(diag_mine[n, pole], lambda d: diag_theirs[d, n])

    def sum_terms(n):
        received(term_copies(n))
        for b, place in batch(n):
            at = (b,) + place
            sums[at] = weighted(res[(b, pole) + place], lambda d: terms[(d,) + at]).astype(BF16)

    def quarter_place(j):
        t = mod(y + j, YN)
        return (slice(None), div(t, 2), mod(t, 2))

    def quarter_copies(j):
        place = quarter_place(j)
        copies = []
        for d in range(1, XN):
            src, dst = (P3, mod(pole + d, XN)) + place, (d - 1, P3) + place
            copies.append(
                remote(
                    res.at[src], terms.at[dst], x_send.at[3, d - 1, j], x_recv.at[3, d - 1, j], pole=mod(pole + d, XN)
                )
            )
        return copies

    def leave_quarter(j):
        received(quarter_copies(j))
        place = quarter_place(j)
        sums[(P3,) + place] = weighted(res[(P3, pole) + place], lambda d: terms[(d, P3) + place]).astype(BF16)
        for p in range(2):
            for side in range(2):
                to = 4 * mod(y + j, YN) + 2 * p + side
                src = sums.at[P3, side, place[1], place[2], p]
                dst = got_d.at[z, :, cols(core, 128)]

                @pl.when(to != row)
                def _():
                    remote(src, dst, o_send.at[3], o_recv.at[3], row=to).start()

                @pl.when(to == row)
                def _():
                    pltpu.make_async_copy(src, dst, o_recv.at[3]).start()

    def batch_copies(n):
        got = gots[n]
        levels = batch(n)
        copies = []
        for d in range(1, 16):
            to = mod((row + d), 16)
            to_z, side = div(to, 2), mod(to, 2)
            src = sums.at[levels[0][0], side, div(to_z, 4), mod((div(to_z, 2)), 2), mod(to_z, 2)]
            copies.append((src, got.at[z, :, cols(core, 128)], to))
        if len(levels) > 1:
            for d in range(1, ZN):
                to_z = mod((z + d), ZN)
                src = sums.at[levels[1][0], core, div(to_z, 4), mod((div(to_z, 2)), 2), mod(to_z, 2)]
                copies.append((src, got.at[ZN + div(z, 2), :, cols(mod(z, 2), 128)], 2 * to_z + core))
        if len(levels) > 2:
            for dh, dp in ((0, 1), (1, 0), (1, 1)):
                h, p = mod((div(z, 4) + dh), 2), mod((z + dp), 2)
                to_z = 4 * h + 2 * fork + p
                src = sums.at[levels[2][0], core, h, fork, p]
                copies.append((src, got.at[ZN + 4 + div(z, 4), :, cols(mod(z, 2), 128)], 2 * to_z + core))
        return [
            remote(src, dst, o_send.at[n], o_recv.at[n], row=to) for src, dst, to in copies
        ]

    def batch_kept(n):
        places = ((z, core), (ZN + div(z, 2), mod(z, 2)), (ZN + 4 + div(z, 4), mod(z, 2)))
        return [
            pltpu.make_async_copy(
                sums.at[b, core, div(z, 4), fork, mod(z, 2)], gots[n].at[at, :, cols(side, 128)], o_recv.at[n]
            )
            for (b, _), (at, side) in zip(batch(n), places)
        ]

    def leave(n):
        start(batch_copies(n) + batch_kept(n))

    def landed(n):
        arrived(gots[n], o_recv.at[n])

    def order(n):
        got = gots[n]

        def with_diagonal(value, node):
            return (value.astype(F32) + diag_sum[node]).astype(BF16)

        if n == 0:
            mine_top[0] = diag_sum[0].astype(BF16)
        for i in range(2):
            if n == 0:
                mine_top[1 + 2 * i] = got[12 + i]
            elif n == 1:
                mine_top[2 + 2 * i] = with_diagonal(got[12 + i], 1 + i)
        for i in range(4):
            if n < 3:
                value = got[8 + place_two[i]]
                mine_two[i, n] = with_diagonal(value, 3 + i) if n == 2 else value
        for k in range(8):
            value = got[place_three[k]]
            mine_three[k // 2, k % 2, n] = with_diagonal(value, 7 + k) if n == 3 else value

    def owner_copies(n):
        copies = []
        for d in range(1, XN):
            to = mod(pole + d, XN)
            pairs = [(mine_three.at[to, :, n], full_three.at[pole, :, n])]
            if n < 3:
                pairs.append((mine_two.at[to, n], full_two.at[pole, n]))
            if n == 1:
                pairs.append((mine_top, full_top.at[pole]))
            for k, (src, dst) in enumerate(pairs):
                copies.append(remote(src, dst, g_send.at[n, d - 1, k], g_recv.at[n, d - 1, k], pole=to))
        return copies

    def to_owner(n):
        landed(n)
        order(n)
        start(owner_copies(n))
        full_three[pole, :, n] = mine_three[pole, :, n]
        if n < 3:
            full_two[pole, n] = mine_two[pole, n]
        if n == 1:
            full_top[pole] = mine_top[...]

    def stage(body):
        lax.fori_loop(0, 4, body, 0)

    mask(L2A)
    pl.semaphore_wait(barrier, 15 + 2 + 3)
    z_start(L2A)
    mask(L2B)
    mask(L1)
    z_sent(L2A)
    z_start(L2B)
    z_start(L1)
    mask(D0)
    mask(L3C)
    gathered(L2A)
    spread(L2A)
    mask(L3B)
    mask(L3A)
    z_sent(L2B)
    z_start(D0)
    gathered(L2B)
    spread(L2B)
    mask(D1)
    mask(D2)
    z_sent(L1)
    z_start(L3C)
    forward(L2A)
    gathered(L1)
    spread(L1)
    mask_diagonals()
    start(diag_copies())
    z_sent(D0)
    z_start(L3B)
    forward(L2B)
    finish(L2A)
    gathered(D0)
    spread(D0)
    z_sent(L3C)
    z_start(L3A)
    forward(L1)
    finish(L2B)
    gathered(L3C)
    spread(L3C)
    z_sent(L3B)
    z_start(D1)
    forward(D0)
    finish(L1)
    gathered(L3B)
    spread(L3B)
    sum_diagonals()
    z_sent(L3A)
    z_start(D2)
    gathered(L3A)
    shared(L2A)
    shared(L2B)
    for b in (L3A, L3B, L3C):
        strip_shared(b)
    stage(first)
    forward(L3C)
    finish(D0)
    z_sent(D1)
    gathered(D1)
    spread(D1)
    shared(L1)
    stage(second)
    z_sent(D2)
    gathered(D2)
    spread(D2)
    spread(L3A)
    shared(D0)
    root_rows()
    start(term_copies(0))
    forward(L3B)
    finish(L3C)
    sum_terms(0)
    leave(0)
    forward(D1)
    finish(D1)
    shared(D1)
    one_rows()
    start(term_copies(1))
    forward(D2)
    finish(L3B)
    finish(D2)
    shared(D2)
    two_rows()
    start(term_copies(2))
    forward(L3A)
    shared(L3B)
    shared(L3C)
    stage(three_begin)
    neighbours_shared(L3A)
    for j in (0, 1, 3):
        three_rows(j)
        start(quarter_copies(j))
    sum_terms(1)
    leave(1)
    finish(L3A)
    to_owner(0)
    across(L3A, 3).wait_recv()
    three_rows(2)
    start(quarter_copies(2))
    for j in (0, 1, 3):
        leave_quarter(j)
    sum_terms(2)
    leave(2)
    leave_quarter(2)
    to_owner(1)
    for b in range(9):
        settle(b)
    sent(diag_copies())
    to_owner(3)
    to_owner(2)
    for n in range(3):
        sent(term_copies(n))
    for j in range(YN):
        sent(quarter_copies(j))
    arrived(mat.at[0:5, 0:5, 0, 0:PART, 0:128], o_send.at[0])
    arrived(mat.at[0:5, 0:5, 0, 0:PART, 0:128], o_send.at[1])
    arrived(got_b.at[0:11], o_send.at[2])
    arrived(mat.at[0:3, 0:5, 0, 0:PART, 0:128], o_send.at[3])
    for n in (0, 1, 3, 2):
        received(owner_copies(n))
        sent(owner_copies(n))


def write(two_ref, three_ref, top_ref, top_out, two_out, three_out):
    for q in range(XN):
        part = slice(q * PART, (q + 1) * PART)
        top_out[:, part] = top_ref[q].astype(F32)
        two_out[0, :, part] = two_ref[q].astype(F32)
        three_out[:, :, part] = three_ref[q].astype(F32)


VMEM = pl.BlockSpec(memory_space=pltpu.VMEM)
SMEM = pl.BlockSpec(memory_space=pltpu.SMEM)
HBM = pl.BlockSpec(memory_space=pltpu.HBM)
GRANT = 58 * 1024 * 1024


def local(
    lower_one,
    lower_two,
    lower_three,
    diag_inverse,
    pole_weight,
    super_sizes,
    parents,
    keep_two,
    keep_three,
):
    one = lower_one.reshape(2, ROWS, COLS)
    two = lower_two.reshape(4, 2, ROWS, COLS)
    three = lower_three.reshape(8, 3, ROWS, COLS)
    diag = diag_inverse.reshape(15, ROWS, COLS)

    dma = pltpu.SemaphoreType.DMA
    parts = pl.pallas_call(
        tree,
        out_shape=(
            jax.ShapeDtypeStruct((XN, 3, PART, COLS), BF16),
            jax.ShapeDtypeStruct((XN, 2, 4, PART, COLS), BF16),
            jax.ShapeDtypeStruct((XN, 5, PART, COLS), BF16),
        ),
        in_specs=[HBM] * 4 + [SMEM] * 5,
        out_specs=(VMEM, VMEM, VMEM),
        scratch_shapes=[
            pltpu.VMEM((2, ROWS, COLS), BF16),
            pltpu.VMEM((4, 2, ROWS, COLS), BF16),
            pltpu.VMEM((8, 3, ROWS, COLS), BF16),
            pltpu.VMEM((15, ROWS, COLS), BF16),
            pltpu.VMEM((ZN, 9, ROWS, COLS), BF16),
            pltpu.VMEM((9, ZN, 2, ROWS, W), BF16),
            pltpu.VMEM((9, XN, 2, 2, 2, 2, PART, 128), BF16),
            pltpu.VMEM((W, 256), F32),
            pltpu.VMEM((W, 256), BF16),
            pltpu.VMEM((384, W), BF16),
            pltpu.VMEM((256, W), BF16),
            pltpu.VMEM((128, W), BF16),
            pltpu.VMEM((128, W), F32),
            pltpu.VMEM((384, W), BF16),
            pltpu.VMEM((256, W), BF16),
            pltpu.VMEM((128, W), BF16),
            pltpu.VMEM((14, PART, COLS), BF16),
            pltpu.VMEM((14, PART, COLS), BF16),
            pltpu.VMEM((12, PART, COLS), BF16),
            pltpu.VMEM((8, PART, COLS), BF16),
            pltpu.VMEM((XN - 1, 9, 2, 2, 2, 2, PART, 128), BF16),
            pltpu.VMEM((9, 2, 2, 2, 2, PART, 128), BF16),
            pltpu.VMEM((15, XN, PART, COLS), BF16),
            pltpu.VMEM((XN - 1, 15, PART, COLS), BF16),
            pltpu.VMEM((15, PART, COLS), F32),
            pltpu.VMEM((XN, 3, PART, COLS), BF16),
            pltpu.VMEM((XN, 2, 4, PART, COLS), BF16),
            pltpu.VMEM((5, PART, COLS), BF16),
            pltpu.VMEM((XN - 1, 8, 128), F32),
            pltpu.VMEM((8, 128), F32),
            dma((4,)),
            dma((9,)),
            dma((9,)),
            dma((9,)),
            dma((9, 2)),
            dma((9, 2)),
            dma((9,)),
            dma((9, 3)),
            dma((3, 3)),
            dma((BATCHES,)),
            dma((BATCHES,)),
            dma((BATCHES, XN - 1, 4)),
            dma((BATCHES, XN - 1, 4)),
            dma((XN - 1, 2)),
            dma((XN - 1, 2)),
            dma((BATCHES, XN - 1, 3)),
            dma((BATCHES, XN - 1, 3)),
        ],
        compiler_params=pltpu.CompilerParams(
            collective_id=0, has_side_effects=True, vmem_limit_bytes=GRANT
        ),
    )(one, two, three, diag, super_sizes.T, parents, keep_two, keep_three.T, pole_weight)

    return pl.pallas_call(
        write,
        out_shape=(
            jax.ShapeDtypeStruct((5, ROWS, COLS), F32),
            jax.ShapeDtypeStruct((1, 3, ROWS, COLS), F32),
            jax.ShapeDtypeStruct((2, 4, ROWS, COLS), F32),
        ),
        in_specs=[VMEM] * 3,
        out_specs=(VMEM, VMEM, VMEM),
    )(*parts)


def solution(mesh):
    placed = (
        P("pole", None, None, "row", "col"),
        P("pole", None, None, "row", "col"),
        P("pole", None, None, "row", "col"),
        P("pole", None, "row", "col"),
        P("pole"),
        P(),
        P(),
        P(),
        P(),
    )
    return jax.shard_map(
        local,
        mesh=mesh,
        in_specs=placed,
        out_specs=(
            P(None, "row", "col"),
            P("pole", None, "row", "col"),
            P("pole", None, "row", "col"),
        ),
        check_vma=False,
    )
```

```python
import jax
import jax.numpy as jnp
from jax import lax
from jax.experimental import pallas as pl
from jax.experimental.pallas import tpu as pltpu
from jax.sharding import PartitionSpec as P

MESH = pl.DeviceIdType.MESH
F32 = jnp.float32
BF16 = jnp.bfloat16
SUPB = 512
W = 1024
ROWS = 64
COLS = 256
ZN = 8
YN = 4
XN = 4

L2A, L2B, L1, D0, D1, D2, L3A, L3B, L3C = range(9)


def mod(a, n):
    return a % n if isinstance(a, int) else lax.rem(a, n)


def div(a, n):
    return a // n if isinstance(a, int) else lax.div(a, n)


def positions(parents_ref):
    two = [parents_ref[i] for i in range(4)]
    three = [parents_ref[4 + k] for k in range(8)]
    place_two = []
    for i in range(4):
        before = sum([(two[h] == two[i]).astype(jnp.int32) for h in range(i)], jnp.int32(0))
        place_two.append(2 * two[i] + before)
    place_three = []
    for k in range(8):
        before = sum([(three[h] == three[k]).astype(jnp.int32) for h in range(k)], jnp.int32(0))
        above = sum([jnp.where(three[k] == i, place_two[i], 0) for i in range(4)], jnp.int32(0))
        place_three.append(2 * above + before)
    return place_two, place_three


def node_at(places, place):
    return sum([jnp.where(p == place, i, 0) for i, p in enumerate(places)], jnp.int32(0))


def limits(sizes_ref):
    row = lax.axis_index("row") * ROWS
    col = lax.axis_index("col") * COLS
    row_sup, row_at = div(row, SUPB), mod(row, SUPB)
    col_sup, col_at = div(col, SUPB), mod(col, SUPB)
    return (lambda n: sizes_ref[row_sup, n] - row_at), (lambda n: sizes_ref[col_sup, n] - col_at)


def below(limit, axis):
    places = lax.broadcasted_iota(jnp.int32, (ROWS, COLS), axis)
    return jnp.where(places < limit, 1.0, 0.0).astype(BF16)


def dot(a, b):
    return jnp.dot(a, b, preferred_element_type=F32)


X3A, X2A, X1, X3B, X2B, P1, X3C, P2, P3 = range(9)
BATCHES = 4
SHARE = {L2A: 2, L2B: 2, L1: 4, D0: 8, D1: 4, D2: 2, L3A: 1, L3B: 1, L3C: 1}
PART = ROWS // XN


def tree(
    one_hbm,
    two_hbm,
    three_hbm,
    diag_hbm,
    sizes_ref,
    parents_ref,
    keep_two_ref,
    keep_three_ref,
    weight_ref,
    full_two,
    full_three,
    full_top,
    one_ref,
    two_ref,
    three_ref,
    diag_ref,
    in_ref,
    mat,
    res,
    yab,
    ybb,
    za,
    zb,
    zc,
    acc,
    yat,
    ybt,
    yct,
    got_a,
    got_b,
    got_c,
    got_d,
    terms,
    sums,
    diag_mine,
    diag_theirs,
    diag_sum,
    mine_two,
    mine_three,
    mine_top,
    weights,
    own_weight,
    load_sem,
    z_send,
    z_recv,
    y_send,
    y_recv,
    f_recv,
    d_send,
    d_recv,
    s_recv,
    o_send,
    o_recv,
    x_send,
    x_recv,
    p_send,
    p_recv,
    g_send,
    g_recv,
):
    pole, row, y = lax.axis_index("pole"), lax.axis_index("row"), lax.axis_index("col")
    z, core = div(row, 2), mod(row, 2)
    other = row + 1 - 2 * core
    up, down = mod((y + 1), YN), mod((y + YN - 1), YN)
    far = mod((y + 2), YN)

    loads = [
        pltpu.make_async_copy(src, dst, load_sem.at[n])
        for n, (src, dst) in enumerate(
            ((two_hbm, two_ref), (one_hbm, one_ref), (diag_hbm, diag_ref), (three_hbm, three_ref))
        )
    ]
    for load in loads:
        load.start()

    barrier = pltpu.get_barrier_semaphore()
    for d in range(1, 16):
        pl.semaphore_signal(barrier, inc=1, device_id={"row": mod((row + d), 16)}, device_id_type=MESH)
    for peer in (up, down):
        pl.semaphore_signal(barrier, inc=1, device_id={"col": peer}, device_id_type=MESH)
    for d in range(1, XN):
        pl.semaphore_signal(barrier, inc=1, device_id={"pole": mod((pole + d), XN)}, device_id_type=MESH)

    place_two, place_three = positions(parents_ref)
    rows_of, cols_of = limits(sizes_ref)
    order_two = [node_at(place_two, j) for j in range(4)]
    order_three = [node_at(place_three, k) for k in range(8)]
    r0, c0 = rows_of(0), cols_of(0)
    r1, c1 = [rows_of(1 + i) for i in range(2)], [cols_of(1 + i) for i in range(2)]
    r2, c2 = [rows_of(3 + n) for n in order_two], [cols_of(3 + n) for n in order_two]
    c3 = [cols_of(7 + n) for n in order_three]
    load_of = {L2A: 0, L2B: 0, L1: 1, D0: 2, D1: 2, D2: 2, L3A: 3, L3B: 3, L3C: 3}

    def block(b, to):
        i, j = div(to, 4), div(to, 2)
        n2, n3 = order_two[j], order_three[to]
        if b == L2A:
            return two_ref[n2, 0] * rows[0] * below(c2[j] * keep_two_ref[n2], 1)
        if b == L2B:
            return two_ref[n2, 1] * rows[1 + i] * below(c2[j], 1)
        if b == L1:
            return one_ref[i] * rows[0] * below(c1[i], 1)
        if b == D0:
            return diag_ref[0] * rows[0] * below(c0, 1)
        if b == D1:
            return diag_ref[1 + i] * rows[1 + i] * below(c1[i], 1)
        if b == D2:
            return diag_ref[3 + n2] * rows[3 + j] * below(c2[j], 1)
        if b == L3A:
            return three_ref[n3, 0] * rows[0] * below(c3[to] * keep_three_ref[0, n3], 1)
        if b == L3B:
            return three_ref[n3, 1] * rows[1 + i] * below(c3[to] * keep_three_ref[1, n3], 1)
        return three_ref[n3, 2] * rows[3 + j] * below(c3[to], 1)

    rows, loaded = {}, set()

    def mask(b):
        if load_of[b] not in loaded:
            loaded.add(load_of[b])
            loads[load_of[b]].wait()
        for n in {L2B: (1, 2), D1: (1, 2), D2: (3, 4, 5, 6), L3B: (1, 2), L3C: (3, 4, 5, 6)}.get(b, (0,)):
            if n not in rows:
                rows[n] = below(r0 if n == 0 else r1[n - 1] if n < 3 else r2[n - 3], 0)
        for to in range(0, ZN, SHARE[b]):
            in_ref[to, b] = block(b, to)

    def cols(at, width=COLS):
        return pl.ds(pl.multiple_of(at * width, width), width)

    def remote(src, dst, send, recv, **device):
        return pltpu.make_async_remote_copy(
            src_ref=src, dst_ref=dst, send_sem=send, recv_sem=recv, device_id=device, device_id_type=MESH
        )

    def along_z(b, d):
        to = mod((z + d), ZN)
        return remote(
            in_ref.at[div(to, SHARE[b]) * SHARE[b], b],
            mat.at[b, z, core, :, cols(y)],
            z_send.at[b],
            z_recv.at[b],
            row=2 * to + core,
        )

    def own_copy(b):
        return pltpu.make_async_copy(
            in_ref.at[div(z, SHARE[b]) * SHARE[b], b], mat.at[b, z, core, :, cols(y)], z_recv.at[b]
        )

    def along_y(b, way, to):
        piece = mat.at[b, :, core, :, cols(y)]
        return remote(piece, piece, y_send.at[b], y_recv.at[b, way], col=to)

    def onward(b, way, source, to):
        piece = mat.at[b, pl.ds(4 * way, 4), core, :, cols(source)]
        return remote(piece, piece, y_send.at[b], f_recv.at[b, way], col=to)

    def across(b, n):
        piece = mat.at[b, :, core, :, cols((y, down, up, far)[n])]
        return remote(piece, piece, d_send.at[b], d_recv.at[b, (0, 1, 1, 2)[n]], row=other)

    def z_start(b):
        own_copy(b).start()
        for d in (4, 3, 5, 2, 6, 1, 7):
            along_z(b, d).start()

    def arrived(ref, sem):
        pltpu.make_async_copy(ref, ref, sem).wait()

    def z_sent(b):
        arrived(mat.at[b, 0 : ZN - 1, core, :, cols(y)], z_send.at[b])

    def gathered(b):
        arrived(mat.at[b, :, core, :, cols(y)], z_recv.at[b])
        across(b, 0).start()

    PIECES = ((1, 1), (2, 1), (3, 3), (2, 3), (1, 3), (2, 2))

    def piece_at(b, i, j):
        return mat.at[b, pl.ds(2 * (mod((y + YN + i), YN)), 2), core, :, cols(mod((y + YN + j), YN))]

    def piece_copy(b, n):
        i, j = PIECES[n]
        if n < 2:
            piece, to = piece_at(b, i - 1, j - 1), down
        elif n < 5:
            piece, to = piece_at(b, i - 3, j - 3), up
        else:
            piece, to = piece_at(b, 1, 1), down
        return remote(piece, piece, y_send.at[b], s_recv.at[b - D0, (0, 1, 1, 1, 1, 2)[n]], col=to)

    def piece_across(b, n):
        piece = piece_at(b, *PIECES[n])
        return remote(piece, piece, d_send.at[b], d_recv.at[b, 1], row=other)

    def spread(b):
        if D0 <= b <= D2:
            for n in (0, 2, 1, 3, 4):
                piece_copy(b, n).start()
            return
        along_y(b, 0, up).start()
        along_y(b, 1, down).start()

    def forward(b):
        if D0 <= b <= D2:
            piece_copy(b, 0).wait_recv()
            piece_copy(b, 5).start()
            arrived(mat.at[b, 0:4, core, :, 0 : 2 * COLS], s_recv.at[b - D0, 1])
            for n in range(5):
                piece_across(b, n).start()
            return
        along_y(b, 0, up).wait_recv()
        onward(b, 0, down, up).start()
        along_y(b, 1, down).wait_recv()
        onward(b, 1, up, down).start()
        across(b, 1).start()
        across(b, 2).start()

    def finish(b):
        if D0 <= b <= D2:
            piece_copy(b, 5).wait_recv()
            piece_across(b, 5).start()
            return
        onward(b, 0, down, up).wait_recv()
        onward(b, 1, up, down).wait_recv()
        across(b, 3).start()

    def strip_shared(b):
        across(b, 0).wait_recv()

    def neighbours_shared(b):
        arrived(mat.at[b, :, core, :, 0 : 2 * COLS], d_recv.at[b, 1])

    def shared(b):
        if b not in (L3A, L3B, L3C):
            strip_shared(b)
        if D0 <= b <= D2:
            arrived(mat.at[b, 0:6, core, :, 0 : 2 * COLS], d_recv.at[b, 1])
        else:
            neighbours_shared(b)
            across(b, 3).wait_recv()

    def settle(b):
        if D0 <= b <= D2:
            arrived(mat.at[b, 0:6, core, :, 0 : 2 * COLS], y_send.at[b])
            arrived(mat.at[b, 0:5, core], d_send.at[b])
        else:
            arrived(mat.at[b, 0:6, core], y_send.at[b])
            arrived(mat.at[b, :, core], d_send.at[b])

    mine = 2 * y + core
    half = 2 * y + mod(z, 2)

    def tall(b, t):
        return mat[b, pl.ds(2 * t, 2)].reshape(256, W)

    def wide(b, t):
        return mat[b, :, :, :, cols(t)].reshape(W, 256)

    def strip(b, at):
        return mat[b, :, :, :, cols(at, 128)].reshape(W, 128)

    def strip_at(b, t, at):
        return mat[b, pl.ds(2 * t, 2), :, :, cols(at, 128)].reshape(256, 128)

    def rows_at(t):
        return pl.ds(pl.multiple_of(t * 256, 256), 256)

    def first(t, carry):
        low = strip(L3C, mine)
        at = rows_at(t)
        yab[at, 0:128] = strip_at(L3A, t, mine).astype(F32) - dot(tall(L2A, t), low)
        yab[at, 128:256] = strip_at(L2A, t, half).astype(F32)
        ybb[at, 0:128] = (strip_at(L3B, t, mine).astype(F32) - dot(tall(L2B, t), low)).astype(BF16)
        ybb[at, 128:256] = strip_at(L2B, t, half)
        return carry

    def second(t, carry):
        at = rows_at(t)
        top = yab[at, :] - dot(tall(L1, t), ybb[...])
        yat[0:256, at] = top.T.astype(BF16)
        yat[256:384, at] = strip_at(L1, t, half).astype(F32).T.astype(BF16)
        ybt[:, at] = ybb[at, :].astype(F32).T.astype(BF16)
        yct[:, at] = strip_at(L3C, t, mine).astype(F32).T.astype(BF16)
        return carry

    def put(n, t, value):
        parts = value.T.astype(BF16).reshape(2, 2, XN, PART, 128)
        for q in range(XN):
            for side in range(2):
                res[n, q, side, div(t, 2), mod(t, 2)] = parts[:, side, q]

    def symmetric(left, b, j):
        value = None
        for i in range(YN):
            at = rows_at(mod((y + i), YN))
            if j == 0 or (i, j) in PIECES:
                piece = mat[b, pl.ds(2 * (mod((y + i), YN)), 2), :, :, cols(mod((y + j), YN))].reshape(COLS, COLS)
                term = dot(left[:, at], piece)
            else:
                piece = mat[b, pl.ds(2 * (mod((y + j), YN)), 2), :, :, cols(mod((y + i), YN))].reshape(COLS, COLS)
                term = lax.dot_general(left[:, at], piece, (((1,), (1,)), ((), ())), preferred_element_type=F32)
            value = term if value is None else value + term
        return value

    def root_rows():
        for j in range(YN):
            t = mod((y + j), YN)
            value = symmetric(yat, D0, j)
            za[:, rows_at(t)] = value.astype(BF16)
            put(X3A, t, -value[0:128])
            put(X2A, t, -value[128:256])
            put(X1, t, -value[256:384])

    def one_rows():
        for j in range(YN):
            t = mod((y + j), YN)
            back = dot(za[...], wide(L1, t))
            value = symmetric(ybt, D1, j) - back[0:256]
            zb[:, rows_at(t)] = value.astype(BF16)
            put(X3B, t, -value[0:128])
            put(X2B, t, -value[128:256])
            put(P1, t, back[256:384])

    def two_rows():
        for j in range(YN):
            t = mod((y + j), YN)
            back = dot(za[0:256, :], wide(L2A, t)) + dot(zb[...], wide(L2B, t))
            value = symmetric(yct, D2, j) - back[0:128]
            zc[:, rows_at(t)] = value.astype(BF16)
            put(X3C, t, -value)
            put(P2, t, back[128:256])

    def three_begin(t, carry):
        acc[:, rows_at(t)] = dot(zb[0:128, :], wide(L3B, t)) + dot(zc[...], wide(L3C, t))
        return carry

    def three_rows(j):
        t = mod(y + j, YN)
        put(P3, t, acc[:, rows_at(t)] + dot(za[0:128, :], wide(L3A, t)))

    gots = (got_a, got_b, got_c, got_d)
    fork = mod((div(z, 2)), 2)

    def batch(n):
        two, one = (core,), (core, slice(None), fork)
        return (
            ((X3A, ()), (X2A, two), (X1, one)),
            ((X3B, ()), (X2B, two), (P1, one)),
            ((X3C, ()), (P2, two)),
        )[n]

    def term_copies(n):
        copies = []
        for d in range(1, XN):
            to = mod((pole + d), XN)
            for k, (b, place) in enumerate(batch(n)):
                copies.append(
                    remote(
                        res.at[(b, to) + place],
                        terms.at[(d - 1, b) + place],
                        x_send.at[n, d - 1, k],
                        x_recv.at[n, d - 1, k],
                        pole=to,
                    )
                )
        return copies

    def diag_copies():
        copies = []
        for d in range(1, XN):
            to = mod((pole + d), XN)
            pairs = ((diag_mine.at[:, to], diag_theirs.at[d - 1]), (own_weight, weights.at[d - 1]))
            for k, (src, dst) in enumerate(pairs):
                copies.append(remote(src, dst, p_send.at[d - 1, k], p_recv.at[d - 1, k], pole=to))
        return copies

    def weighted(own, others):
        value = weight_ref[0] * own.astype(F32)
        for d in range(XN - 1):
            value = value + weights[d, 0:1, 0:1] * others(d).astype(F32)
        return value

    def start(copies):
        for copy in copies:
            copy.start()

    def sent(copies):
        for copy in copies:
            copy.wait_send()

    def received(copies):
        for copy in copies:
            copy.wait_recv()

    def mask_diagonals():
        own_weight[...] = jnp.full((8, 128), weight_ref[0], F32)
        for n in range(15):
            live = below(rows_of(n), 0) * below(cols_of(n), 1)
            diag_mine[n] = (diag_ref[n] * live).reshape(XN, PART, COLS)

    def sum_diagonals():
        received(diag_copies())
        for n in range(15):
            diag_sum[n] = weighted(diag_mine[n, pole], lambda d: diag_theirs[d, n])

    def sum_terms(n):
        received(term_copies(n))
        for b, place in batch(n):
            at = (b,) + place
            sums[at] = weighted(res[(b, pole) + place], lambda d: terms[(d,) + at]).astype(BF16)

    def quarter_place(j):
        t = mod(y + j, YN)
        return (slice(None), div(t, 2), mod(t, 2))

    def quarter_copies(j):
        place = quarter_place(j)
        copies = []
        for d in range(1, XN):
            src, dst = (P3, mod(pole + d, XN)) + place, (d - 1, P3) + place
            copies.append(
                remote(
                    res.at[src], terms.at[dst], x_send.at[3, d - 1, j], x_recv.at[3, d - 1, j], pole=mod(pole + d, XN)
                )
            )
        return copies

    def leave_quarter(j):
        received(quarter_copies(j))
        place = quarter_place(j)
        sums[(P3,) + place] = weighted(res[(P3, pole) + place], lambda d: terms[(d, P3) + place]).astype(BF16)
        for p in range(2):
            for side in range(2):
                to = 4 * mod(y + j, YN) + 2 * p + side
                src = sums.at[P3, side, place[1], place[2], p]
                dst = got_d.at[z, :, cols(core, 128)]

                @pl.when(to != row)
                def _():
                    remote(src, dst, o_send.at[3], o_recv.at[3], row=to).start()

                @pl.when(to == row)
                def _():
                    pltpu.make_async_copy(src, dst, o_recv.at[3]).start()

    def batch_copies(n):
        got = gots[n]
        levels = batch(n)
        copies = []
        for d in range(1, 16):
            to = mod((row + d), 16)
            to_z, side = div(to, 2), mod(to, 2)
            src = sums.at[levels[0][0], side, div(to_z, 4), mod((div(to_z, 2)), 2), mod(to_z, 2)]
            copies.append((src, got.at[z, :, cols(core, 128)], to))
        if len(levels) > 1:
            for d in range(1, ZN):
                to_z = mod((z + d), ZN)
                src = sums.at[levels[1][0], core, div(to_z, 4), mod((div(to_z, 2)), 2), mod(to_z, 2)]
                copies.append((src, got.at[ZN + div(z, 2), :, cols(mod(z, 2), 128)], 2 * to_z + core))
        if len(levels) > 2:
            for dh, dp in ((0, 1), (1, 0), (1, 1)):
                h, p = mod((div(z, 4) + dh), 2), mod((z + dp), 2)
                to_z = 4 * h + 2 * fork + p
                src = sums.at[levels[2][0], core, h, fork, p]
                copies.append((src, got.at[ZN + 4 + div(z, 4), :, cols(mod(z, 2), 128)], 2 * to_z + core))
        return [
            remote(src, dst, o_send.at[n], o_recv.at[n], row=to) for src, dst, to in copies
        ]

    def batch_kept(n):
        places = ((z, core), (ZN + div(z, 2), mod(z, 2)), (ZN + 4 + div(z, 4), mod(z, 2)))
        return [
            pltpu.make_async_copy(
                sums.at[b, core, div(z, 4), fork, mod(z, 2)], gots[n].at[at, :, cols(side, 128)], o_recv.at[n]
            )
            for (b, _), (at, side) in zip(batch(n), places)
        ]

    def leave(n):
        start(batch_copies(n) + batch_kept(n))

    def landed(n):
        arrived(gots[n], o_recv.at[n])

    def order(n):
        got = gots[n]

        def with_diagonal(value, node):
            return (value.astype(F32) + diag_sum[node]).astype(BF16)

        if n == 0:
            mine_top[0] = diag_sum[0].astype(BF16)
        for i in range(2):
            if n == 0:
                mine_top[1 + 2 * i] = got[12 + i]
            elif n == 1:
                mine_top[2 + 2 * i] = with_diagonal(got[12 + i], 1 + i)
        for i in range(4):
            if n < 3:
                value = got[8 + place_two[i]]
                mine_two[i, n] = with_diagonal(value, 3 + i) if n == 2 else value
        for k in range(8):
            value = got[place_three[k]]
            mine_three[k // 2, k % 2, n] = with_diagonal(value, 7 + k) if n == 3 else value

    def owner_copies(n):
        copies = []
        for d in range(1, XN):
            to = mod(pole + d, XN)
            pairs = [(mine_three.at[to, :, n], full_three.at[pole, :, n])]
            if n < 3:
                pairs.append((mine_two.at[to, n], full_two.at[pole, n]))
            if n == 1:
                pairs.append((mine_top, full_top.at[pole]))
            for k, (src, dst) in enumerate(pairs):
                copies.append(remote(src, dst, g_send.at[n, d - 1, k], g_recv.at[n, d - 1, k], pole=to))
        return copies

    def to_owner(n):
        landed(n)
        order(n)
        start(owner_copies(n))
        full_three[pole, :, n] = mine_three[pole, :, n]
        if n < 3:
            full_two[pole, n] = mine_two[pole, n]
        if n == 1:
            full_top[pole] = mine_top[...]

    def stage(body):
        lax.fori_loop(0, 4, body, 0)

    mask(L2A)
    pl.semaphore_wait(barrier, 15 + 2 + 3)
    z_start(L2A)
    mask(L2B)
    mask(L1)
    z_sent(L2A)
    z_start(L2B)
    z_start(L1)
    mask(D0)
    mask(L3C)
    gathered(L2A)
    spread(L2A)
    mask(L3B)
    mask(L3A)
    z_sent(L2B)
    z_start(D0)
    gathered(L2B)
    spread(L2B)
    mask(D1)
    mask(D2)
    z_sent(L1)
    z_start(L3C)
    forward(L2A)
    gathered(L1)
    spread(L1)
    mask_diagonals()
    start(diag_copies())
    z_sent(D0)
    z_start(L3B)
    forward(L2B)
    finish(L2A)
    gathered(D0)
    spread(D0)
    z_sent(L3C)
    z_start(L3A)
    forward(L1)
    finish(L2B)
    gathered(L3C)
    spread(L3C)
    z_sent(L3B)
    z_start(D1)
    forward(D0)
    finish(L1)
    gathered(L3B)
    spread(L3B)
    sum_diagonals()
    z_sent(L3A)
    z_start(D2)
    gathered(L3A)
    shared(L2A)
    shared(L2B)
    for b in (L3A, L3B, L3C):
        strip_shared(b)
    stage(first)
    forward(L3C)
    finish(D0)
    z_sent(D1)
    gathered(D1)
    spread(D1)
    shared(L1)
    stage(second)
    z_sent(D2)
    gathered(D2)
    spread(D2)
    spread(L3A)
    shared(D0)
    root_rows()
    start(term_copies(0))
    forward(L3B)
    finish(L3C)
    sum_terms(0)
    leave(0)
    forward(D1)
    finish(D1)
    shared(D1)
    one_rows()
    start(term_copies(1))
    forward(D2)
    finish(L3B)
    finish(D2)
    shared(D2)
    two_rows()
    start(term_copies(2))
    forward(L3A)
    shared(L3B)
    shared(L3C)
    stage(three_begin)
    neighbours_shared(L3A)
    for j in (0, 1, 3):
        three_rows(j)
        start(quarter_copies(j))
    sum_terms(1)
    leave(1)
    finish(L3A)
    across(L3A, 3).wait_recv()
    three_rows(2)
    start(quarter_copies(2))
    to_owner(0)
    for j in (0, 1, 3):
        leave_quarter(j)
    sum_terms(2)
    leave(2)
    leave_quarter(2)
    to_owner(1)
    for b in range(9):
        settle(b)
    sent(diag_copies())
    to_owner(3)
    to_owner(2)
    for n in range(3):
        sent(term_copies(n))
    for j in range(YN):
        sent(quarter_copies(j))
    arrived(mat.at[0:5, 0:5, 0, 0:PART, 0:128], o_send.at[0])
    arrived(mat.at[0:5, 0:5, 0, 0:PART, 0:128], o_send.at[1])
    arrived(got_b.at[0:11], o_send.at[2])
    arrived(mat.at[0:3, 0:5, 0, 0:PART, 0:128], o_send.at[3])
    for n in (0, 1, 3, 2):
        received(owner_copies(n))
        sent(owner_copies(n))


def write(two_ref, three_ref, top_ref, top_out, two_out, three_out):
    for q in range(XN):
        part = slice(q * PART, (q + 1) * PART)
        top_out[:, part] = top_ref[q].astype(F32)
        two_out[0, :, part] = two_ref[q].astype(F32)
        three_out[:, :, part] = three_ref[q].astype(F32)


VMEM = pl.BlockSpec(memory_space=pltpu.VMEM)
SMEM = pl.BlockSpec(memory_space=pltpu.SMEM)
HBM = pl.BlockSpec(memory_space=pltpu.HBM)
GRANT = 58 * 1024 * 1024


def local(
    lower_one,
    lower_two,
    lower_three,
    diag_inverse,
    pole_weight,
    super_sizes,
    parents,
    keep_two,
    keep_three,
):
    one = lower_one.reshape(2, ROWS, COLS)
    two = lower_two.reshape(4, 2, ROWS, COLS)
    three = lower_three.reshape(8, 3, ROWS, COLS)
    diag = diag_inverse.reshape(15, ROWS, COLS)

    dma = pltpu.SemaphoreType.DMA
    parts = pl.pallas_call(
        tree,
        out_shape=(
            jax.ShapeDtypeStruct((XN, 3, PART, COLS), BF16),
            jax.ShapeDtypeStruct((XN, 2, 4, PART, COLS), BF16),
            jax.ShapeDtypeStruct((XN, 5, PART, COLS), BF16),
        ),
        in_specs=[HBM] * 4 + [SMEM] * 5,
        out_specs=(VMEM, VMEM, VMEM),
        scratch_shapes=[
            pltpu.VMEM((2, ROWS, COLS), BF16),
            pltpu.VMEM((4, 2, ROWS, COLS), BF16),
            pltpu.VMEM((8, 3, ROWS, COLS), BF16),
            pltpu.VMEM((15, ROWS, COLS), BF16),
            pltpu.VMEM((ZN, 9, ROWS, COLS), BF16),
            pltpu.VMEM((9, ZN, 2, ROWS, W), BF16),
            pltpu.VMEM((9, XN, 2, 2, 2, 2, PART, 128), BF16),
            pltpu.VMEM((W, 256), F32),
            pltpu.VMEM((W, 256), BF16),
            pltpu.VMEM((384, W), BF16),
            pltpu.VMEM((256, W), BF16),
            pltpu.VMEM((128, W), BF16),
            pltpu.VMEM((128, W), F32),
            pltpu.VMEM((384, W), BF16),
            pltpu.VMEM((256, W), BF16),
            pltpu.VMEM((128, W), BF16),
            pltpu.VMEM((14, PART, COLS), BF16),
            pltpu.VMEM((14, PART, COLS), BF16),
            pltpu.VMEM((12, PART, COLS), BF16),
            pltpu.VMEM((8, PART, COLS), BF16),
            pltpu.VMEM((XN - 1, 9, 2, 2, 2, 2, PART, 128), BF16),
            pltpu.VMEM((9, 2, 2, 2, 2, PART, 128), BF16),
            pltpu.VMEM((15, XN, PART, COLS), BF16),
            pltpu.VMEM((XN - 1, 15, PART, COLS), BF16),
            pltpu.VMEM((15, PART, COLS), F32),
            pltpu.VMEM((XN, 3, PART, COLS), BF16),
            pltpu.VMEM((XN, 2, 4, PART, COLS), BF16),
            pltpu.VMEM((5, PART, COLS), BF16),
            pltpu.VMEM((XN - 1, 8, 128), F32),
            pltpu.VMEM((8, 128), F32),
            dma((4,)),
            dma((9,)),
            dma((9,)),
            dma((9,)),
            dma((9, 2)),
            dma((9, 2)),
            dma((9,)),
            dma((9, 3)),
            dma((3, 3)),
            dma((BATCHES,)),
            dma((BATCHES,)),
            dma((BATCHES, XN - 1, 4)),
            dma((BATCHES, XN - 1, 4)),
            dma((XN - 1, 2)),
            dma((XN - 1, 2)),
            dma((BATCHES, XN - 1, 3)),
            dma((BATCHES, XN - 1, 3)),
        ],
        compiler_params=pltpu.CompilerParams(
            collective_id=0, has_side_effects=True, vmem_limit_bytes=GRANT
        ),
    )(one, two, three, diag, super_sizes.T, parents, keep_two, keep_three.T, pole_weight)

    return pl.pallas_call(
        write,
        out_shape=(
            jax.ShapeDtypeStruct((5, ROWS, COLS), F32),
            jax.ShapeDtypeStruct((1, 3, ROWS, COLS), F32),
            jax.ShapeDtypeStruct((2, 4, ROWS, COLS), F32),
        ),
        in_specs=[VMEM] * 3,
        out_specs=(VMEM, VMEM, VMEM),
    )(*parts)


def solution(mesh):
    placed = (
        P("pole", None, None, "row", "col"),
        P("pole", None, None, "row", "col"),
        P("pole", None, None, "row", "col"),
        P("pole", None, "row", "col"),
        P("pole"),
        P(),
        P(),
        P(),
        P(),
    )
    return jax.shard_map(
        local,
        mesh=mesh,
        in_specs=placed,
        out_specs=(
            P(None, "row", "col"),
            P("pole", None, "row", "col"),
            P("pole", None, "row", "col"),
        ),
        check_vma=False,
    )
```
